512 devices in a mesh: prow: 32 (over z, x), pcol: 16 (over y, core).
Axes of the slice: x: 4, y: 8, z: 8, core: 2. Of those that a mesh axis runs over, the one named last changes fastest.
Arguments:
- matrix: float32 [61440, 4096], P('prow', 'pcol'), may hold values from -6 to 6
- pivots: int32 [2, 64], replicated, may hold values from 64 to 61439, as said below
- lower_inv: float32 [2, 64, 64], replicated, may hold values from -0.5 to 1, as said below
- upper_inv: float32 [2, 64, 64], replicated, may hold values from -0.1 to 0.1, as said below
Outputs:
- factored: float32 [61440, 4096], P('prow', 'pcol')
The draws below stay inside these ranges and needn't reach their ends.
Inputs may be any that keep to these rules, and one draw needn't show every extreme that they name: `pivots`: row k holds 64 different global rows, all at least 64 * (k + 1); it contains 64 * (k + 1) and 61439, and every process row holds at least one of them. `lower_inv`: each matrix is unit lower triangular. `upper_inv`: each matrix is upper triangular with diagonal entries between 0.05 and 0.1.
All inputs are finite; a program needn't handle non-finite values.
Results may differ from the reference program's by a relative error of at most 0.0051.
Values may be sent and summed in bfloat16 or wider, within the bound.
A program may use at most 64 MiB of HBM per device.

```python
import jax
import jax.numpy as jnp
from jax import lax

NB = 64
STEPS = 2
ROWS_DEV = 1920
COLS_DEV = 256
ROWS = 61440
COLS = 4096


def draw_pivots(key, part):
    key = jax.random.fold_in(key, 11)
    proc_rows = ROWS // ROWS_DEV
    local_blocks = ROWS_DEV // NB
    chosen = []
    for panel_step in range(STEPS):
        start = (panel_step + 1) * NB
        sub_key = jax.random.fold_in(key, panel_step)
        block_key = jax.random.fold_in(sub_key, 2)
        offset_key = jax.random.fold_in(sub_key, 3)
        rest_key = jax.random.fold_in(sub_key, 4)
        order_key = jax.random.fold_in(sub_key, 5)
        devices = [p for p in range(proc_rows) if p != panel_step + 1 and p != proc_rows - 1]
        device_ids = jnp.array(devices, dtype=jnp.int32)
        local_pick = jax.random.randint(block_key, (len(devices),), 1, local_blocks, dtype=jnp.int32)
        offset_pick = jax.random.randint(offset_key, (len(devices),), 0, NB, dtype=jnp.int32)
        per_device = (local_pick * proc_rows + device_ids) * NB + offset_pick
        pool_start = (panel_step + 2) * NB
        pool_size = (proc_rows - panel_step - 2) * NB
        rest = jax.random.permutation(rest_key, pool_size)[:NB - proc_rows].astype(jnp.int32) + pool_start
        both_ends = jnp.array([start, ROWS - 1], dtype=jnp.int32)
        entries = jnp.concatenate([per_device.astype(jnp.int32), rest, both_ends])
        chosen.append(jax.random.permutation(order_key, entries))
    return jnp.stack(chosen).astype(jnp.int32)


def draw_lower_inv(key, part):
    key = jax.random.fold_in(key, 23)
    positions = jnp.arange(NB)
    strict_lower = (positions[:, None] > positions[None, :]).astype(jnp.float32)
    entries = 0.1 * jax.random.normal(key, (STEPS, NB, NB), jnp.float32)
    entries = jnp.clip(entries, -0.5, 0.5)
    return entries * strict_lower + jnp.eye(NB, dtype=jnp.float32)


def draw_upper_inv(key, part):
    key = jax.random.fold_in(key, 37)
    diag_key, off_key = jax.random.split(key)
    positions = jnp.arange(NB)
    strict_upper = (positions[:, None] < positions[None, :]).astype(jnp.float32)
    diagonal_part = jax.random.uniform(diag_key, (STEPS, NB), jnp.float32, 0.05, 0.1)
    entries = 0.0125 * jax.random.normal(off_key, (STEPS, NB, NB), jnp.float32)
    entries = jnp.clip(entries, -0.1, 0.1)
    return entries * strict_upper + diagonal_part[:, :, None] * jnp.eye(NB, dtype=jnp.float32)


def steps_of(own_key, shape, cuts, smallest, largest):
    def one(dim, shards_of):
        heights = jax.random.uniform(jax.random.fold_in(jax.random.fold_in(own_key, 6), dim), (shards_of,), jnp.float32, smallest / len(cuts), largest / len(cuts))
        return jnp.repeat(jnp.exp(heights), shape[dim] // shards_of).reshape((-1,) + (1,) * (len(shape) - dim - 1))

    loudness = one(*cuts[0])
    for cut in cuts[1:]:
        loudness = loudness * one(*cut)
    return loudness


def bell_draw(rng, shape, spread, most, cuts=(), held_as=jnp.bfloat16):
    level = steps_of(rng, shape, cuts, -0.22, 0.18) if cuts else 1.0
    values = jax.random.normal(rng, shape, jnp.float32) * spread * level
    return jnp.minimum(jnp.maximum(values, -most), most).astype(held_as)


def setup_inputs(seed: int = 0) -> dict:
    arg_keys = jax.random.split(jax.random.key(seed), 5)
    return {
        "matrix": bell_draw(arg_keys[0], (ROWS, COLS), 1.0, 6.0, ((0, 32), (1, 16)), jnp.float32),
        "pivots": draw_pivots(jax.random.fold_in(arg_keys[4], 71), 0),
        "lower_inv": draw_lower_inv(jax.random.fold_in(arg_keys[4], 71), 0),
        "upper_inv": draw_upper_inv(jax.random.fold_in(arg_keys[4], 71), 0),
    }


def position_of(global_rows, per_dev, dev_count):
    block_ids = global_rows // NB
    return ((block_ids % dev_count) * per_dev + (block_ids // dev_count) * NB + global_rows % NB).astype(jnp.int32)


def blocks_of(extent, per_dev, dev_count):
    positions = jnp.arange(extent, dtype=jnp.int32)
    return (((positions % per_dev) // NB) * dev_count + positions // per_dev).astype(jnp.int32)


def reference(matrix, pivots, lower_inv, upper_inv):
    prow_count = ROWS // ROWS_DEV
    pcol_count = COLS // COLS_DEV
    row_blocks = blocks_of(ROWS, ROWS_DEV, prow_count)
    col_blocks = blocks_of(COLS, COLS_DEV, pcol_count)
    offsets = jnp.arange(NB, dtype=jnp.int32)
    current = matrix
    for panel_step in range(STEPS):
        top_index = position_of(panel_step * NB + offsets, ROWS_DEV, prow_count)
        pivot_index = position_of(pivots[panel_step].astype(jnp.int32), ROWS_DEV, prow_count)
        panel_index = position_of(panel_step * NB + offsets, COLS_DEV, pcol_count)
        top_values = current[top_index]
        pivot_values = current[pivot_index]
        current = current.at[top_index].set(pivot_values).at[pivot_index].set(top_values)
        row_below = (row_blocks > panel_step)[:, None]
        col_right = (col_blocks > panel_step)[None, :]
        panel_cols = current[:, panel_index]
        lower_cols = jnp.where(row_below, jnp.dot(panel_cols, upper_inv[panel_step], precision=lax.Precision.HIGHEST), 0.0)
        upper_rows = jnp.where(col_right, jnp.dot(lower_inv[panel_step], pivot_values, precision=lax.Precision.HIGHEST), 0.0)
        current = current.at[:, panel_index].set(jnp.where(row_below, lower_cols, panel_cols))
        current = current.at[top_index].set(jnp.where(col_right, upper_rows, pivot_values))
        product = jnp.dot(lower_cols.astype(jnp.bfloat16), upper_rows.astype(jnp.bfloat16), preferred_element_type=jnp.float32)
        current = current - product
    return current
```

```python
import functools

import jax
import jax.numpy as jnp
from jax import lax
from jax.experimental import pallas as pl
from jax.experimental.pallas import tpu as pltpu
from jax.sharding import PartitionSpec as P

NB = 64
LANES = 128
HIGHEST = lax.Precision.HIGHEST
MESH = pl.DeviceIdType.MESH


def dot(a, b, precision=None):
    return jnp.dot(a, b, precision=precision, preferred_element_type=jnp.float32)


def left_of(x):
    lane = lax.broadcasted_iota(jnp.int32, x.shape, 1)
    return jnp.where(lane < NB, x, jnp.zeros_like(x))


def right_of(x):
    lane = lax.broadcasted_iota(jnp.int32, x.shape, 1)
    return jnp.where(lane < NB, jnp.zeros_like(x), x)


def exchange(np_, nq, loc, hold, matrix, upper, lower, special, panels, fixes,
             here, send1, recv1, tops, tops_in, load_sem, send_sem, recv_sem, top_sem):
    me_p, me_q = lax.axis_index("prow"), lax.axis_index("pcol")
    ny = nq // 2
    me_y, me_c = me_q // 2, me_q % 2
    rows = here.shape[0]
    per = NB // np_
    height = panels.shape[1]
    chunk = height // ny
    wide = here.shape[1] // LANES
    deep = 4 * per * wide

    def at(p, q):
        return dict(device_id=(p, q), device_id_type=MESH)

    load = pltpu.make_async_copy(matrix, here, load_sem)
    load.start()
    barrier = pltpu.get_barrier_semaphore()

    def greet_p(d, _):
        pl.semaphore_signal(barrier, inc=1, **at(lax.rem(me_p + d, np_), me_q))
        return 0

    def greet_q(d, _):
        pl.semaphore_signal(barrier, inc=1, **at(me_p, lax.rem(me_q + d, nq)))
        return 0

    lax.fori_loop(1, np_, greet_p, 0)
    lax.fori_loop(1, nq, greet_q, 0)
    load.wait()

    def fill(r, _):
        for step in range(2):
            for s in range(per):
                row = loc[step, r + s * np_]
                send1[r, pl.ds(step * per + s, 1), :] = here[pl.ds(row, 1), :]
        return 0

    lax.fori_loop(0, np_, fill, 0)
    recv1[np_ - 1] = send1[me_p]

    @pl.when(me_p < 2)
    def _():
        def fill_top(r, _):
            for s in range(per):
                tops[r, pl.ds(s, 1), :] = here[pl.ds(r + s * np_, 1), :]
            return 0

        lax.fori_loop(0, np_, fill_top, 0)
        tops_in[me_p] = tops[me_p]

    pl.semaphore_wait(barrier, np_ + nq - 2)

    def start1(d, _):
        to = lax.rem(me_p + d, np_)
        pltpu.make_async_remote_copy(
            send1.at[to], recv1.at[d - 1], send_sem.at[0], recv_sem.at[0], **at(to, me_q)
        ).start()
        return 0

    lax.fori_loop(1, np_, start1, 0)

    @pl.when(me_p < 2)
    def _():
        def start_top(d, _):
            to = lax.rem(me_p + d, np_)
            pltpu.make_async_remote_copy(
                tops.at[to], tops_in.at[me_p], send_sem.at[1], top_sem.at[me_p], **at(to, me_q)
            ).start()
            return 0

        lax.fori_loop(1, np_, start_top, 0)

    def panel_part(c, y):
        return panels.at[c, pl.ds(pl.multiple_of(y * chunk, chunk), chunk)]

    @pl.when(me_y == 0)
    def _():
        both = upper[me_c]
        for begin in range(0, height, LANES):
            part = dot(here[pl.ds(begin, LANES), :NB], both[:, :LANES], HIGHEST)
            if begin + height < rows:
                part += dot(here[pl.ds(height + begin, LANES), :NB], both[:, LANES:], HIGHEST)
            panels[me_c, pl.ds(begin, LANES), :] = part.astype(jnp.bfloat16)

        def start_part(y, _):
            pltpu.make_async_remote_copy(
                panel_part(me_c, y), panel_part(me_c, y), send_sem.at[2], recv_sem.at[2],
                **at(me_p, 2 * y + me_c)
            ).start()
            return 0

        lax.fori_loop(1, ny, start_part, 0)

    pltpu.make_async_remote_copy(
        recv1.at[pl.ds(0, np_ - 1)], recv1.at[pl.ds(0, np_ - 1)], send_sem.at[0], recv_sem.at[0],
        **at(me_p, me_q)
    ).wait_recv()
    for step in range(2):
        @pl.when(me_p != step)
        def _():
            pltpu.make_async_remote_copy(
                tops.at[0], tops_in.at[step], send_sem.at[1], top_sem.at[step], **at(me_p, me_q)
            ).wait_recv()

    mine = pl.multiple_of(me_p * deep, deep)
    for step in range(2):
        for s in range(per):
            slot = lax.rem(me_p - hold[step, me_p + s * np_] - 1 + 2 * np_, np_)
            pivot_row = recv1[slot, pl.ds(step * per + s, 1), :]
            top_row = tops_in[step, pl.ds(s, 1), :]
            for w in range(wide):
                lanes = slice(w * LANES, (w + 1) * LANES)
                special[pl.ds(mine + (step * per + s) * wide + w, 1), :] = pivot_row[:, lanes]
                special[pl.ds(mine + ((2 + step) * per + s) * wide + w, 1), :] = top_row[:, lanes]

    def start2(d, _):
        to = lax.rem(me_p + d, np_)
        pltpu.make_async_remote_copy(
            special.at[pl.ds(mine, deep)], special.at[pl.ds(mine, deep)],
            send_sem.at[3], recv_sem.at[3], **at(to, me_q)
        ).start()
        return 0

    lax.fori_loop(1, np_, start2, 0)

    @pl.when(me_y > 0)
    def _():
        pltpu.make_async_remote_copy(
            panel_part(me_c, me_y), panel_part(me_c, me_y), send_sem.at[2], recv_sem.at[2],
            **at(me_p, me_q)
        ).wait_recv()

    def start_pass(d, _):
        to = lax.rem(me_y + d, ny)

        @pl.when(to > 0)
        def _():
            pltpu.make_async_remote_copy(
                panel_part(me_c, me_y), panel_part(me_c, me_y), send_sem.at[4], recv_sem.at[4],
                **at(me_p, 2 * to + me_c)
            ).start()
        return 0

    lax.fori_loop(1, ny, start_pass, 0)

    def to_sibling():
        return pltpu.make_async_remote_copy(
            panels.at[me_c], panels.at[me_c], send_sem.at[5], recv_sem.at[5],
            **at(me_p, 2 * me_y + 1 - me_c)
        )

    @pl.when(me_y == 0)
    def _():
        to_sibling().start()

    pltpu.make_async_remote_copy(
        special.at[pl.ds(0, deep * (np_ - 1))], special.at[pl.ds(0, deep * (np_ - 1))],
        send_sem.at[3], recv_sem.at[3], **at(me_p, me_q)
    ).wait_recv()

    @pl.when(me_y == 0)
    def _():
        def some(kind, s):
            return special[pl.ds((kind * per + s) * wide, np_, stride=deep), :][:, :NB]

        both = upper[me_c]
        top = [jnp.concatenate([some(kind, s) for s in range(per)], 0) for kind in range(4)]
        part = dot(top[2], both[:, :LANES], HIGHEST) + dot(top[3], both[:, LANES:], HIGHEST)
        fixes[me_c, :NB, :] = part.astype(jnp.bfloat16)
        half = NB // 2

        @pl.when(me_c == 0)
        def _():
            part = dot(top[1][:half], both[:, :LANES], HIGHEST) + dot(top[1][half:], both[:, LANES:], HIGHEST)
            fixes[0, NB:, :] = part.astype(jnp.bfloat16)

        @pl.when(me_c == 1)
        def _():
            part = dot(lower[0], top[0], HIGHEST)
            part = jnp.concatenate([part[:half], part[half:]], 1)
            fixes[1, NB:, :] = part.astype(jnp.bfloat16)

        def start3(d, _):
            pltpu.make_async_remote_copy(
                fixes.at[me_c], fixes.at[me_c], send_sem.at[6], top_sem.at[2 + me_c],
                **at(me_p, lax.rem(me_q + d, nq))
            ).start()
            return 0

        lax.fori_loop(1, nq, start3, 0)

    @pl.when(me_y > 0)
    def _():
        parts = panels.at[me_c, pl.ds(0, chunk * (ny - 1))]
        pltpu.make_async_remote_copy(
            parts, parts, send_sem.at[4], recv_sem.at[4], **at(me_p, me_q)
        ).wait_recv()
        to_sibling().start()

    to_sibling().wait()
    for c in range(2):
        @pl.when(me_q != c)
        def _():
            pltpu.make_async_remote_copy(
                fixes.at[c], fixes.at[c], send_sem.at[6], top_sem.at[2 + c], **at(me_p, me_q)
            ).wait_recv()

    def sent(ref, sem):
        pltpu.make_async_remote_copy(ref, ref, sem, recv_sem.at[0], **at(me_p, me_q)).wait_send()

    sent(send1.at[pl.ds(0, np_ - 1)], send_sem.at[0])

    @pl.when(me_p < 2)
    def _():
        sent(tops.at[pl.ds(0, np_ - 1)], send_sem.at[1])

    sent(special.at[pl.ds(0, deep * (np_ - 1))], send_sem.at[3])

    @pl.when(me_y == 0)
    def _():
        sent(panels.at[0, pl.ds(0, chunk * (ny - 1))], send_sem.at[2])
        sent(panels.at[0, pl.ds(0, chunk * (ny - 1))], send_sem.at[4])

        def sent_fix(d, _):
            sent(fixes.at[0], send_sem.at[6])
            return 0

        lax.fori_loop(1, nq, sent_fix, 0)

    @pl.when(me_y > 0)
    def _():
        if ny > 2:
            sent(panels.at[0, pl.ds(0, chunk * (ny - 2))], send_sem.at[4])


def update(np_, places, same, lower, upper, special, panels, fixes, matrix, out):
    me_p, me_q = lax.axis_index("prow"), lax.axis_index("pcol")
    rows, cols = matrix.shape
    height = panels.shape[1]
    per = NB // np_
    half = NB // 2
    bf16 = jnp.bfloat16

    wide = cols // LANES

    def rows_of(kind):
        def part(s, w):
            return special[pl.ds((kind * per + s) * wide + w, np_, stride=4 * per * wide), :]

        return jnp.concatenate(
            [jnp.concatenate([part(s, w) for s in range(per)], 0) for w in range(wide)], 1
        )

    pivot0, pivot1, top0, top1 = (rows_of(kind) for kind in range(4))
    lane = lax.broadcasted_iota(jnp.int32, (NB, cols), 1)
    row = lax.broadcasted_iota(jnp.int32, (NB, cols), 0)
    in_panel = lane < NB

    upper0 = dot(lower[0], pivot0, HIGHEST)
    half0 = upper0.astype(bf16)
    moved = same[...].astype(jnp.float32)
    stays = 1.0 - jnp.sum(moved, axis=1, keepdims=True)
    pivot1 = pivot1 * stays + dot(moved, top0, HIGHEST)
    fix0, fix1 = fixes[0, :NB, :].astype(jnp.float32), fixes[1, :NB, :].astype(jnp.float32)

    def unpack(x):
        x = x.astype(jnp.float32)
        return jnp.concatenate([x[:, :NB], x[:, NB:]], 0)

    left1 = unpack(fixes[0, NB:, :])
    left1 = left1 * stays + dot(moved, fix0[:, :NB])
    rest1 = pivot1 - dot(left1.astype(bf16), half0)
    upper1 = dot(lower[1], rest1, HIGHEST)
    half1 = upper1.astype(bf16)
    cross = dot(unpack(fixes[1, NB:, :]), upper[1][:, :LANES], HIGHEST)
    cross = jnp.concatenate([cross, pltpu.roll(cross, NB, 1)], 0)
    cross_hi = cross.astype(bf16)
    cross_lo = (cross - cross_hi.astype(jnp.float32)).astype(bf16)

    unit = jnp.where(lane == row, -1.0, 0.0).astype(bf16)
    none = jnp.zeros_like(unit)
    here0, here1 = in_panel & (me_q == 0), in_panel & (me_q == 1)
    right0 = jnp.where(here0, unit, jnp.where(here1, none, half0))
    right1 = jnp.where(here1, unit, jnp.where(here0, none, half1))
    keep_row = jnp.where((here0 | here1)[:1], 0.0, 1.0)

    tops = jnp.concatenate([top0, top1], 0) * keep_row
    tops_hi = tops.astype(bf16)
    tops_lo = (tops - tops_hi.astype(jnp.float32)).astype(bf16)
    keep_all = jnp.broadcast_to(keep_row, (2 * NB, cols)).astype(bf16)
    place = places[...]

    def panel_tops(fix, ones):
        left = jnp.concatenate([left_of(fix), left_of(pltpu.roll(fix, NB, 1))], 0)
        right = jnp.concatenate([right_of(pltpu.roll(fix, NB, 1)), right_of(fix)], 0)
        return left.astype(bf16), right.astype(bf16)

    left_a, right_a = panel_tops(fix0, 0)
    left_b, right_b = panel_tops(fix1, 0)
    ones = jnp.ones((2 * NB, LANES), bf16)
    left_all = jnp.concatenate([left_a, left_b, left_of(ones)], 1)
    right_all = jnp.concatenate([right_a, right_b, right_of(ones)], 1)

    def placed(begin):
        local = begin + lax.broadcasted_iota(jnp.int32, (LANES, 2 * NB), 0)
        whole = (local // NB * np_ + me_p) * NB + local % NB
        return jnp.where(whole == place, 1.0, 0.0).astype(bf16)

    for begin in range(0, height, LANES):
        place_l = placed(begin)
        both = dot(place_l, left_all)
        two = begin + height < rows
        if two:
            place_r = placed(height + begin)
            both += dot(place_r, right_all)
        stay = 1.0 - both[:, 2 * LANES:]
        panel0 = panels[0, pl.ds(begin, LANES), :].astype(jnp.float32) * stay + both[:, :LANES]
        panel1 = panels[1, pl.ds(begin, LANES), :].astype(jnp.float32) * stay + both[:, LANES:2 * LANES]
        panel0 = panel0.astype(bf16)
        panel1 = (panel1 - dot(panel0, cross_hi) - dot(panel0, cross_lo)).astype(bf16)
        for side in range(2 if two else 1):
            put = place_r if side else place_l
            at = pl.ds(side * height + begin, LANES)
            zero = jnp.zeros_like(right0)
            pad = (lambda x: jnp.concatenate([zero, x], 0)) if side else (lambda x: jnp.concatenate([x, zero], 0))
            value = matrix[at, :] * (keep_row - dot(put, keep_all)) + dot(put, tops_hi) + dot(put, tops_lo)
            value -= dot(panel0, pad(right0))
            value -= dot(panel1, pad(right1))
            out[at, :] = value

    @pl.when(me_p == 0)
    def _():
        out[:NB, :] = jnp.where(here0, pivot0, upper0)

    @pl.when(me_p == 1)
    def _():
        wide = jnp.concatenate([left1] * (cols // NB), 1)
        out[:NB, :] = jnp.where(here0, wide, jnp.where(here1, rest1, upper1))


def local(np_, nq, matrix, pivots, lower_inv, upper_inv):
    rows, cols = matrix.shape
    ny = nq // 2
    per = NB // np_
    chunk = -(-rows // (2 * ny * LANES)) * LANES
    height = chunk * ny
    block = pivots // NB
    hold = block % np_
    loc = block // np_ * NB + pivots % NB
    nothing = jnp.zeros_like(upper_inv)
    upper = jnp.concatenate([upper_inv, nothing, nothing, upper_inv], 2)

    first, second = pivots[0], pivots[1]
    same = second[:, None] == first[None, :]
    low = (NB + jnp.arange(NB, dtype=jnp.int32))[:, None] == first[None, :]
    via = jnp.sum(jnp.where(low, second[:, None], 0), 0)
    place0 = jnp.where(jnp.any(low, 0), via, jnp.where(jnp.any(same, 0), -1, first))
    place1 = jnp.where(jnp.any(low, 1), -1, second)
    places = jnp.concatenate([place0, place1])[None, :]

    vmem = pl.BlockSpec(memory_space=pltpu.VMEM)
    smem = pl.BlockSpec(memory_space=pltpu.SMEM)
    special, panels, fixes = pl.pallas_call(
        functools.partial(exchange, np_, nq),
        out_shape=(
            jax.ShapeDtypeStruct((4 * NB * (cols // LANES), LANES), jnp.float32),
            jax.ShapeDtypeStruct((2, height, LANES), jnp.bfloat16),
            jax.ShapeDtypeStruct((2, NB + NB // 2, LANES), jnp.bfloat16),
        ),
        in_specs=[smem, smem, pl.BlockSpec(memory_space=pl.ANY), vmem, vmem],
        out_specs=(vmem, vmem, vmem),
        scratch_shapes=[
            pltpu.VMEM((rows, cols), jnp.float32),
            pltpu.VMEM((np_, 2 * per, cols), jnp.float32),
            pltpu.VMEM((np_, 2 * per, cols), jnp.float32),
            pltpu.VMEM((np_, per, cols), jnp.float32),
            pltpu.VMEM((2, per, cols), jnp.float32),
            pltpu.SemaphoreType.DMA,
            pltpu.SemaphoreType.DMA((7,)),
            pltpu.SemaphoreType.DMA((6,)),
            pltpu.SemaphoreType.DMA((4,)),
        ],
        compiler_params=pltpu.CompilerParams(
            collective_id=0, has_side_effects=True, vmem_limit_bytes=32 * 1024 * 1024
        ),
    )(loc, hold, matrix, upper, lower_inv)
    return pl.pallas_call(
        functools.partial(update, np_),
        out_shape=jax.ShapeDtypeStruct((rows, cols), jnp.float32),
        in_specs=[vmem] * 8,
        out_specs=vmem,
        compiler_params=pltpu.CompilerParams(vmem_limit_bytes=32 * 1024 * 1024),
    )(places, same.astype(jnp.float32), lower_inv, upper, special, panels, fixes, matrix)


def solution(mesh):
    placed = (P("prow", "pcol"), P(), P(), P())
    return jax.shard_map(
        functools.partial(local, mesh.shape["prow"], mesh.shape["pcol"]),
        mesh=mesh, in_specs=placed, out_specs=P("prow", "pcol"), check_vma=False,
    )
```

```python
import functools

import jax
import jax.numpy as jnp
from jax import lax
from jax.experimental import pallas as pl
from jax.experimental.pallas import tpu as pltpu
from jax.sharding import PartitionSpec as P

NB = 64
LANES = 128
HIGHEST = lax.Precision.HIGHEST
MESH = pl.DeviceIdType.MESH
BF16 = jnp.bfloat16
VMEM_LIMIT = 32 * 1024 * 1024


def dot(a, b, precision=None):
    return jnp.dot(a, b, precision=precision, preferred_element_type=jnp.float32)


def iota(shape, axis):
    return lax.broadcasted_iota(jnp.int32, shape, axis)


def beside(x, side):
    parts = [x, jnp.zeros_like(x)]
    return jnp.concatenate(parts[::-1] if side else parts, 1)


def column(row):
    on = iota((NB, NB), 0) == iota((NB, NB), 1)
    return jnp.sum(jnp.where(on, row, jnp.zeros_like(row)), axis=1, keepdims=True)


def pivot_maps(pivots):
    values = pivots[...].astype(jnp.float32)
    first, second = values[0:1], values[1:2]
    same = (column(second) == first).astype(jnp.float32)
    low = ((NB + iota((NB, NB), 0)).astype(jnp.float32) == first).astype(jnp.float32)
    return first, second, same, low


def spread(x):
    high = x.astype(BF16)
    return high, (x - high.astype(jnp.float32)).astype(BF16)


def exchange(np_, nx, nq, scalars, pivots_at, matrix, lower_at, upper_at, base, put, heads, panels, pieces, pivots, lower, upper,
             special, send1, recv1, tops, tops_in, send_z, recv_z, recv_y, load_sem, sends, recvs):
    me_p, me_q = lax.axis_index("prow"), lax.axis_index("pcol")
    ny, nz = nq // 2, np_ // nx
    me_y, me_c = lax.div(me_q, 2), lax.rem(me_q, 2)
    me_z, me_x = lax.div(me_p, nx), lax.rem(me_p, nx)
    rows, cols = base.shape
    per, group = NB // np_, NB // nz
    height = panels.shape[1]
    quarter = height // 4
    wide = cols // LANES
    deep = 4 * per * wide

    def at(p, q):
        return dict(device_id=(p, q), device_id_type=MESH)

    def remote(src, dst, send, recv, p, q):
        return pltpu.make_async_remote_copy(src, dst, sends.at[send], recvs.at[recv], **at(p, q))

    def arrived(ref, recv):
        remote(ref, ref, 0, recv, me_p, me_q).wait_recv()

    def sent(ref, send):
        remote(ref, ref, send, 0, me_p, me_q).wait_send()

    def each(lower_, upper_, do):
        def body(d, _):
            do(d)
            return 0

        lax.fori_loop(lower_, upper_, body, 0)

    def place(step, i):
        value = scalars[step, i]
        block = lax.div(value, NB)
        return lax.div(block, np_) * NB + lax.rem(value, NB)

    def holder(step, i):
        return lax.rem(lax.div(scalars[step, i], NB), np_)

    loads = [
        pltpu.make_async_copy(src, dst, load_sem.at[k])
        for k, (src, dst) in enumerate(((pivots_at, pivots), (matrix, base), (upper_at, upper), (lower_at, lower)))
    ]
    for load in loads:
        load.start()
    barrier = pltpu.get_barrier_semaphore()
    each(1, np_, lambda d: pl.semaphore_signal(barrier, inc=1, **at(lax.rem(me_p + d, np_), me_q)))
    each(1, nq, lambda d: pl.semaphore_signal(barrier, inc=1, **at(me_p, lax.rem(me_q + d, nq))))

    loads[0].wait()
    first, second, same, low = pivot_maps(pivots)
    gone = (first < 2 * NB) | (jnp.sum(same, axis=0, keepdims=True) > 0)
    goal = jnp.concatenate([jnp.where(gone, -1.0, first), second], 1).astype(jnp.int32)
    for begin in range(0, rows, LANES):
        mine_rows = begin + iota((LANES, 2 * NB), 0)
        whole = (lax.div(mine_rows, NB) * np_ + me_p) * NB + lax.rem(mine_rows, NB)
        put[pl.ds(begin, LANES), :] = jnp.where(whole == goal, 1.0, 0.0).astype(BF16)
    for load in loads[1:]:
        load.wait()

    def fill(r):
        for step in range(2):
            for s in range(per):
                send1[r, pl.ds(step * per + s, 1), :] = base[pl.ds(place(step, r + s * np_), 1), :]

    each(0, np_, fill)
    recv1[np_ - 1] = send1[me_p]

    @pl.when(me_p < 2)
    def _():
        def fill_top(r):
            for s in range(per):
                tops[r, pl.ds(s, 1), :] = base[pl.ds(r + s * np_, 1), :]

        each(0, np_, fill_top)
        tops_in[me_p] = tops[me_p]

    @pl.when(me_y == 0)
    def _():
        mine = upper[me_c]
        left, right = beside(mine, 0), beside(mine, 1)

        def fill_z(z):
            for g in range(group):
                row = place(1 - me_c, z * group + g)
                send_z[z, pl.ds(g, 1), :] = base[pl.ds(row, 1), :][:, :LANES]

        each(0, nz, fill_z)
        some = send_z[...].reshape(NB, LANES)
        lane = iota((NB, LANES), 1)
        first_part = jnp.where(me_c == 0, dot(some[:, :NB], left, HIGHEST), jnp.where(lane < NB, some, 0.0))
        both = first_part + dot(base[:NB, :NB], right, HIGHEST)
        send_z[...] = both.reshape(nz, group, LANES)
        recv_z[me_z] = send_z[me_z]
        for begin in range(0, height, LANES):
            part = dot(base[pl.ds(begin, LANES), :NB], left, HIGHEST)
            if begin + height < rows:
                part += dot(base[pl.ds(height + begin, LANES), :NB], right, HIGHEST)
            panels[me_c, pl.ds(begin, LANES), :] = part.astype(BF16)

    pl.semaphore_wait(barrier, np_ + nq - 2)

    def panel(c, k, begin=0, size=quarter):
        return panels.at[c, pl.ds(pl.multiple_of(k * quarter + begin, 16), size)]

    def pass_on(y, begin, size):
        to = lax.rem(me_y + y + ny, ny)

        @pl.when(to > 0)
        def _():
            part = panel(me_c, lax.rem(me_y, 4), begin, size)
            remote(part, part, 5, 5, me_p, 2 * to + me_c).start()

    def pass_on_all():
        half = quarter // 2
        pass_on(2, 0, half)
        pass_on(-2, half, half)
        pass_on(1, 0, quarter)
        pass_on(-1, 0, quarter)

    def to_sibling(part):
        remote(part, part, 6, 6, me_p, 2 * me_y + 1 - me_c).start()

    @pl.when(me_y == 0)
    def _():
        def start_z(d):
            to = lax.rem(me_z + d, nz)
            remote(send_z.at[to], recv_z.at[me_z], 0, 0, to * nx + me_x, me_q).start()

        each(1, nz, start_z)
        for d in range(ny // 2, 0, -1):
            for y in sorted({d, ny - d}):
                part = panel(me_c, y % 4)
                remote(part, part, 4, 4, me_p, 2 * y + me_c).start()

    def start1(d):
        to = lax.rem(me_p + d, np_)
        remote(send1.at[to], recv1.at[d - 1], 1, 1, to, me_q).start()

    each(1, np_, start1)

    @pl.when(me_p < 2)
    def _():
        def start_top(d):
            to = lax.rem(me_p + d, np_)
            remote(tops.at[to], tops_in.at[me_p], 2, 9 + me_p, to, me_q).start()

        each(1, np_, start_top)

    @pl.when(me_y == 0)
    def _():
        pass_on_all()
        to_sibling(panels.at[me_c])
        arrived(recv_z.at[pl.ds(0, nz - 1)], 0)
        lane = iota((1, LANES), 1)
        for g in range(group):
            z = lax.div(holder(1 - me_c, me_z * group + g), nx)
            row = jnp.where(lane < NB, recv_z[z, pl.ds(g, 1), :], recv_z[0, pl.ds(g, 1), :])
            recv_y[me_c, pl.ds(g, 1), :] = row
        each(1, nq, lambda d: remote(recv_y.at[me_c], recv_y.at[me_c], 7, 7 + me_c,
                                     me_p, lax.rem(me_q + d, nq)).start())

    @pl.when(me_y > 0)
    def _():
        arrived(panel(me_c, lax.rem(me_y, 4)), 4)
        pass_on_all()
        to_sibling(panel(me_c, lax.rem(me_y, 4)))

    arrived(recv1.at[pl.ds(0, np_ - 1)], 1)
    for step in range(2):
        @pl.when(me_p != step)
        def _():
            arrived(tops_in.at[step], 9 + step)

    mine = pl.multiple_of(me_p * deep, deep)
    for step in range(2):
        for s in range(per):
            slot = lax.rem(me_p - holder(step, me_p + s * np_) - 1 + 2 * np_, np_)
            pivot_row = recv1[slot, pl.ds(step * per + s, 1), :]
            top_row = tops_in[step, pl.ds(s, 1), :]
            for w in range(wide):
                lanes = slice(w * LANES, (w + 1) * LANES)
                special[pl.ds(mine + (step * per + s) * wide + w, 1), :] = pivot_row[:, lanes]
                special[pl.ds(mine + ((2 + step) * per + s) * wide + w, 1), :] = top_row[:, lanes]

    own = special.at[pl.ds(mine, deep)]
    each(1, np_, lambda d: remote(own, own, 3, 3, lax.rem(me_p + d, np_), me_q).start())

    for c in range(2):
        @pl.when(me_q != c)
        def _():
            arrived(recv_y.at[c], 7 + c)

    begin = pl.multiple_of(me_p * (2 * group), 2 * group)
    pieces[pl.ds(begin, 2 * group), :] = recv_y[...].reshape(2 * group, LANES).astype(BF16)
    piece = pieces.at[pl.ds(begin, 2 * group)]
    each(1, np_, lambda d: remote(piece, piece, 8, 2, lax.rem(me_p + d, np_), me_q).start())

    @pl.when(me_y > 0)
    def _():
        arrived(panels.at[me_c, pl.ds(0, 3 * quarter)], 5)
        for k in range(1, 4):
            to_sibling(panel(me_c, lax.rem(me_y + k, 4)))

    arrived(special.at[pl.ds(0, deep * (np_ - 1))], 3)

    def rows_of(kind):
        def part(s, w):
            return special[pl.ds((kind * per + s) * wide + w, np_, stride=deep), :]

        return jnp.concatenate(
            [jnp.concatenate([part(s, w) for s in range(per)], 0) for w in range(wide)], 1
        )

    pivot0, pivot1, top0, top1 = (rows_of(kind) for kind in range(4))
    heads[:NB, :] = pivot0
    heads[NB:2 * NB, :] = dot(lower[0], pivot0, HIGHEST)
    stays = 1.0 - jnp.sum(same, axis=1, keepdims=True)
    heads[2 * NB:, :] = pivot1 * stays + dot(same, top0, HIGHEST)
    stays = 1.0 - jnp.sum(low, axis=1, keepdims=True)
    top1 = top1 * stays + dot(low, top0, HIGHEST)
    change = jnp.concatenate([top0 - pivot0, top1 - pivot1], 0)
    change = jnp.concatenate(spread(change), 0)
    for begin_ in range(0, rows, LANES):
        take = put[pl.ds(begin_, LANES), :]
        base[pl.ds(begin_, LANES), :] += dot(jnp.concatenate([take, take], 1), change)

    arrived(pieces.at[pl.ds(0, 2 * group * (np_ - 1))], 2)
    arrived(panels.at[1 - me_c], 6)

    sent(send1.at[pl.ds(0, np_ - 1)], 1)
    sent(special.at[pl.ds(0, deep * (np_ - 1))], 3)
    sent(pieces.at[pl.ds(0, 2 * group * (np_ - 1))], 8)
    sent(panels.at[me_c], 6)

    @pl.when(me_p < 2)
    def _():
        sent(tops.at[pl.ds(0, np_ - 1)], 2)

    @pl.when(me_y == 0)
    def _():
        sent(send_z.at[pl.ds(0, nz - 1)], 0)
        each(1, ny, lambda d: sent(panel(0, 0), 4))
        each(1, nq, lambda d: sent(recv_y.at[0], 7))

    near = (me_y == 1) | (me_y == ny - 1)
    far = (me_y == 2) | (me_y == ny - 2)
    sent(panels.at[0, pl.ds(0, 2 * quarter)], 5)

    @pl.when(~near)
    def _():
        sent(panels.at[0, pl.ds(0, quarter // 2)], 5)

    @pl.when(~(near | far))
    def _():
        sent(panels.at[0, pl.ds(0, quarter // 2)], 5)


def update(np_, nx, base, put, heads, panels, pieces, pivots, lower, upper, out, held, out_sem):
    me_p, me_q = lax.axis_index("prow"), lax.axis_index("pcol")
    rows, cols = base.shape
    height = panels.shape[1]
    nz = np_ // nx
    group = NB // nz
    pivot0, upper0, head1 = (heads[pl.ds(k * NB, NB), :] for k in range(3))
    lane, row = iota((NB, cols), 1), iota((NB, cols), 0)
    in_panel = lane < NB
    here0, here1 = in_panel & (me_q == 0), in_panel & (me_q == 1)

    first, second, same, low = pivot_maps(pivots)
    stays = 1.0 - jnp.sum(same, axis=1, keepdims=True)
    stays_low = 1.0 - jnp.sum(low, axis=1, keepdims=True)
    same, low = same.astype(BF16), low.astype(BF16)

    def part(x, c):
        return pieces[...].astype(jnp.float32).reshape(nz, nx, 2, group, LANES)[:, x, c].reshape(NB, LANES)

    def held_at(row_of, c):
        x_of = lax.rem(lax.div(column(row_of).astype(jnp.int32), NB), nx)
        value = part(0, c)
        for x in range(1, nx):
            value = jnp.where(x_of == x, part(x, c), value)
        return value[:, :NB]

    def tops_of(c):
        top0, top1 = part(0, c)[:, NB:], part(1, c)[:, NB:]
        return top0, top1 * stays_low + dot(low, top0.astype(BF16))

    panel_tops = [tops_of(c) for c in range(2)]

    left1 = held_at(second, 0) * stays + dot(same, panel_tops[0][0].astype(BF16))
    half0 = upper0.astype(BF16)
    rest1 = head1 - dot(left1.astype(BF16), half0)
    upper1 = dot(lower[1], rest1, HIGHEST)
    half1 = upper1.astype(BF16)

    cross = dot(lower[0], held_at(first, 1), HIGHEST).astype(BF16).astype(jnp.float32)
    cross = dot(cross, upper[1], HIGHEST)
    cross = jnp.concatenate([beside(cross, 0), beside(cross, 1)], 0)
    cross = jnp.concatenate(spread(cross), 0)

    unit = jnp.where(lane == row, -1.0, 0.0).astype(BF16)
    none = jnp.zeros_like(unit)
    right0 = jnp.where(here0, unit, jnp.where(here1, none, half0))
    right1 = jnp.where(here1, unit, jnp.where(here0, none, half1))
    keep = jnp.where((here0 | here1)[:1], 0.0, 1.0)
    rights = (
        jnp.concatenate([right0, none, right1, none], 0),
        jnp.concatenate([none, right0, none, right1], 0),
    )
    ones = jnp.ones((2 * NB, NB), jnp.float32)

    def moved(side):
        parts = [jnp.concatenate(panel_tops[c], 0) for c in range(2)] + [ones]
        return jnp.concatenate([beside(x, side) for x in parts], 1).astype(BF16)

    moved0, moved1 = moved(0), moved(1)
    copies = []
    step = 4 * LANES
    for begin in range(0, height, step):
        size = min(step, height - begin)
        over = max(0, min(size, rows - height - begin))
        both = dot(put[pl.ds(begin, size), :], moved0)
        if over:
            side1 = dot(put[pl.ds(height + begin, over), :], moved1)
            if over < size:
                side1 = jnp.concatenate([side1, jnp.zeros((size - over, 3 * LANES), jnp.float32)], 0)
            both += side1
        stay = 1.0 - both[:, 2 * LANES:]
        panel0 = panels[0, pl.ds(begin, size), :].astype(jnp.float32) * stay + both[:, :LANES]
        panel1 = panels[1, pl.ds(begin, size), :].astype(jnp.float32) * stay + both[:, LANES:2 * LANES]
        panel0 = panel0.astype(BF16)
        panel1 = (panel1 - dot(jnp.concatenate([panel0, panel0], 1), cross)).astype(BF16)
        two = jnp.concatenate([panel0, panel1], 1)
        for side, count in ((0, size), (1, over)):
            if count:
                where = pl.ds(side * height + begin, count)
                held[where, :] = base[where, :] * keep - dot(two[:count], rights[side])
                if side == 0 and begin == 0:
                    @pl.when(me_p == 0)
                    def _():
                        held[:NB, :] = jnp.where(here0, pivot0, upper0)

                    @pl.when(me_p == 1)
                    def _():
                        wide = jnp.concatenate([left1] * (cols // NB), 1)
                        held[:NB, :] = jnp.where(here0, wide, jnp.where(here1, rest1, upper1))

                copies.append(pltpu.make_async_copy(held.at[where], out.at[where], out_sem.at[len(copies)]))
                copies[-1].start()
    for copy in copies:
        copy.wait()


def local(np_, nx, nq, matrix, pivots, lower_inv, upper_inv):
    rows, cols = matrix.shape
    nz = np_ // nx
    per, group = NB // np_, NB // nz
    height = -(-rows // (2 * LANES)) * LANES
    vmem = pl.BlockSpec(memory_space=pltpu.VMEM)
    smem = pl.BlockSpec(memory_space=pltpu.SMEM)
    anywhere = pl.BlockSpec(memory_space=pl.ANY)
    f32 = jnp.float32
    kept = pl.pallas_call(
        functools.partial(exchange, np_, nx, nq),
        out_shape=(
            jax.ShapeDtypeStruct((rows, cols), f32),
            jax.ShapeDtypeStruct((rows, 2 * NB), BF16),
            jax.ShapeDtypeStruct((3 * NB, cols), f32),
            jax.ShapeDtypeStruct((2, height, LANES), BF16),
            jax.ShapeDtypeStruct((np_ * 2 * group, LANES), BF16),
            jax.ShapeDtypeStruct(pivots.shape, jnp.int32),
            jax.ShapeDtypeStruct(lower_inv.shape, f32),
            jax.ShapeDtypeStruct(upper_inv.shape, f32),
        ),
        in_specs=[smem] + [anywhere] * 4,
        out_specs=(vmem,) * 8,
        scratch_shapes=[
            pltpu.VMEM((4 * NB * (cols // LANES), LANES), f32),
            pltpu.VMEM((np_, 2 * per, cols), f32),
            pltpu.VMEM((np_, 2 * per, cols), f32),
            pltpu.VMEM((np_, per, cols), f32),
            pltpu.VMEM((2, per, cols), f32),
            pltpu.VMEM((nz, group, LANES), f32),
            pltpu.VMEM((nz, group, LANES), f32),
            pltpu.VMEM((2, group, LANES), f32),
            pltpu.SemaphoreType.DMA((4,)),
            pltpu.SemaphoreType.DMA((9,)),
            pltpu.SemaphoreType.DMA((11,)),
        ],
        compiler_params=pltpu.CompilerParams(
            collective_id=0, has_side_effects=True, vmem_limit_bytes=VMEM_LIMIT
        ),
    )(pivots, *(pltpu.with_memory_space_constraint(x, pltpu.HBM) for x in (pivots, matrix, lower_inv, upper_inv)))
    return pl.pallas_call(
        functools.partial(update, np_, nx),
        out_shape=jax.ShapeDtypeStruct((rows, cols), f32),
        in_specs=[vmem] * 8,
        out_specs=anywhere,
        scratch_shapes=[pltpu.VMEM((rows, cols), f32), pltpu.SemaphoreType.DMA((2 * height // LANES,))],
        compiler_params=pltpu.CompilerParams(vmem_limit_bytes=VMEM_LIMIT),
    )(*kept)


def solution(mesh):
    np_, nq = mesh.shape["prow"], mesh.shape["pcol"]
    nx = 4 if np_ > 4 else 2
    placed = (P("prow", "pcol"), P(), P(), P())
    return jax.shard_map(
        functools.partial(local, np_, nx, nq),
        mesh=mesh, in_specs=placed, out_specs=P("prow", "pcol"), check_vma=False,
    )
```

```python
import functools

import jax
import jax.numpy as jnp
from jax import lax
from jax.experimental import pallas as pl
from jax.experimental.pallas import tpu as pltpu
from jax.sharding import PartitionSpec as P

NB = 64
LANES = 128
HIGHEST = lax.Precision.HIGHEST
MESH = pl.DeviceIdType.MESH
BF16 = jnp.bfloat16
VMEM_LIMIT = 32 * 1024 * 1024


def dot(a, b, precision=None):
    return jnp.dot(a, b, precision=precision, preferred_element_type=jnp.float32)


def iota(shape, axis):
    return lax.broadcasted_iota(jnp.int32, shape, axis)


def beside(x, side):
    parts = [x, jnp.zeros_like(x)]
    return jnp.concatenate(parts[::-1] if side else parts, 1)


def column(row):
    on = iota((NB, NB), 0) == iota((NB, NB), 1)
    return jnp.sum(jnp.where(on, row, jnp.zeros_like(row)), axis=1, keepdims=True)


def pivot_maps(pivots):
    values = pivots[...].astype(jnp.float32)
    first, second = values[0:1], values[1:2]
    same = (column(second) == first).astype(jnp.float32)
    low = ((NB + iota((NB, NB), 0)).astype(jnp.float32) == first).astype(jnp.float32)
    return first, second, same, low


def spread(x):
    high = x.astype(BF16)
    return high, (x - high.astype(jnp.float32)).astype(BF16)


def exchange(np_, nx, nq, scalars, pivots_at, matrix, lower_at, upper_at, base, put, heads, panels, pieces, pivots, lower, upper,
             special, send1, recv1, tops, tops_all, send_z, recv_z, picked, recv_y, load_sem, sends, recvs):
    me_p, me_q = lax.axis_index("prow"), lax.axis_index("pcol")
    ny, nz = nq // 2, np_ // nx
    me_y, me_c = lax.div(me_q, 2), lax.rem(me_q, 2)
    me_z, me_x = lax.div(me_p, nx), lax.rem(me_p, nx)
    rows, cols = base.shape
    per, group = NB // np_, NB // nz
    height = panels.shape[1]
    quarter = height // 4
    wide = cols // LANES
    deep = 2 * per * wide

    def at(p, q):
        return dict(device_id=(p, q), device_id_type=MESH)

    def remote(src, dst, send, recv, p, q):
        return pltpu.make_async_remote_copy(src, dst, sends.at[send], recvs.at[recv], **at(p, q))

    def arrived(ref, recv):
        remote(ref, ref, 0, recv, me_p, me_q).wait_recv()

    def sent(ref, send):
        remote(ref, ref, send, 0, me_p, me_q).wait_send()

    def each(lower_, upper_, do):
        def body(d, _):
            do(d)
            return 0

        lax.fori_loop(lower_, upper_, body, 0)

    def place(step, i):
        value = scalars[step, i]
        block = lax.div(value, NB)
        return lax.div(block, np_) * NB + lax.rem(value, NB)

    def holder(step, i):
        return lax.rem(lax.div(scalars[step, i], NB), np_)

    loads = [
        pltpu.make_async_copy(src, dst, load_sem.at[k])
        for k, (src, dst) in enumerate(((pivots_at, pivots), (matrix, base), (upper_at, upper), (lower_at, lower)))
    ]
    for load in loads:
        load.start()
    barrier = pltpu.get_barrier_semaphore()
    each(1, np_, lambda d: pl.semaphore_signal(barrier, inc=1, **at(lax.rem(me_p + d, np_), me_q)))
    each(1, nq, lambda d: pl.semaphore_signal(barrier, inc=1, **at(me_p, lax.rem(me_q + d, nq))))

    loads[0].wait()
    first, second, same, low = pivot_maps(pivots)
    gone = (first < 2 * NB) | (jnp.sum(same, axis=0, keepdims=True) > 0)
    goal = jnp.concatenate([jnp.where(gone, -1.0, first), second], 1).astype(jnp.int32)
    for begin in range(0, rows, LANES):
        mine_rows = begin + iota((LANES, 2 * NB), 0)
        whole = (lax.div(mine_rows, NB) * np_ + me_p) * NB + lax.rem(mine_rows, NB)
        put[pl.ds(begin, LANES), :] = jnp.where(whole == goal, 1.0, 0.0).astype(BF16)
    for load in loads[1:]:
        load.wait()

    def fill(r):
        for step in range(2):
            for s in range(per):
                send1[r, pl.ds(step * per + s, 1), :] = base[pl.ds(place(step, r + s * np_), 1), :]

    each(0, np_, fill)
    recv1[np_ - 1] = send1[me_p]

    @pl.when(me_p < 2)
    def _():
        parts = [base[:NB, w * LANES:(w + 1) * LANES].reshape(nz, group, LANES) for w in range(wide)]
        tops[...] = jnp.concatenate(parts, 1).astype(BF16)
        tops_all[me_z, me_p] = tops[me_z]

    @pl.when(me_y == 0)
    def _():
        mine = upper[me_c]
        left, right = beside(mine, 0), beside(mine, 1)

        def fill_z(z):
            for g in range(group):
                row = place(1 - me_c, z * group + g)
                send_z[z, pl.ds(g, 1), :] = base[pl.ds(row, 1), :][:, :LANES]

        each(0, nz, fill_z)
        some = send_z[...].reshape(NB, LANES)
        lane = iota((NB, LANES), 1)
        first_part = jnp.where(me_c == 0, dot(some[:, :NB], left, HIGHEST), jnp.where(lane < NB, some, 0.0))
        both = first_part + dot(base[:NB, :NB], right, HIGHEST)
        send_z[...] = both.reshape(nz, group, LANES)
        recv_z[me_p] = send_z[me_z]
        for begin in range(0, height, LANES):
            part = dot(base[pl.ds(begin, LANES), :NB], left, HIGHEST)
            if begin + height < rows:
                part += dot(base[pl.ds(height + begin, LANES), :NB], right, HIGHEST)
            panels[me_c, pl.ds(begin, LANES), :] = part.astype(BF16)

    pl.semaphore_wait(barrier, np_ + nq - 2)

    def panel(c, k, begin=0, size=quarter):
        return panels.at[c, pl.ds(pl.multiple_of(k * quarter + begin, 16), size)]

    def pass_on(y, begin, size):
        to = lax.rem(me_y + y + ny, ny)

        @pl.when(to > 0)
        def _():
            part = panel(me_c, lax.rem(me_y, 4), begin, size)
            remote(part, part, 5, 5, me_p, 2 * to + me_c).start()

    def pass_on_all():
        half = quarter // 2
        pass_on(2, 0, half)
        pass_on(-2, half, half)
        pass_on(1, 0, quarter)
        pass_on(-1, 0, quarter)

    def to_sibling(part):
        remote(part, part, 6, 6, me_p, 2 * me_y + 1 - me_c).start()

    @pl.when(me_y == 0)
    def _():
        def start_z(d):
            to = lax.rem(me_p + d, np_)
            remote(send_z.at[lax.div(to, nx)], recv_z.at[me_p], 0, 0, to, me_q).start()

        each(1, np_, start_z)

    def start1(d):
        to = lax.rem(me_p + d, np_)
        remote(send1.at[to], recv1.at[d - 1], 1, 1, to, me_q).start()

    each(1, np_, start1)

    @pl.when(me_p < 2)
    def _():
        def start_top(d):
            to = lax.rem(me_p + d, np_)
            to_z = lax.div(to, nx)
            remote(tops.at[to_z], tops_all.at[to_z, me_p], 2, 9 + me_p, to, me_q).start()

        each(1, np_, start_top)

    @pl.when(me_y == 0)
    def _():
        for d in range(ny // 2, 0, -1):
            for y in sorted({d, ny - d}):
                part = panel(me_c, y % 4)
                remote(part, part, 4, 4, me_p, 2 * y + me_c).start()
        pass_on_all()
        to_sibling(panels.at[me_c])
        arrived(recv_z.at[pl.ds(0, np_ - 1)], 0)
        lane = iota((group, LANES), 1)
        for g in range(group):
            row = recv_z[holder(1 - me_c, me_z * group + g), pl.ds(g, 1), :]
            picked[pl.ds(g, 1), :] = row
        value = picked[...]
        high = value.astype(BF16).astype(jnp.float32)
        upper_half = jnp.where(lane < NB, value, recv_z[0])
        lower_half = jnp.where(lane < NB, pltpu.roll(recv_z[1], NB, 1), pltpu.roll(value - high, NB, 1))
        recv_y[me_c] = jnp.concatenate([upper_half, lower_half], 0).astype(BF16)
        each(1, nq, lambda d: remote(recv_y.at[me_c], recv_y.at[me_c], 7, 7 + me_c,
                                     me_p, lax.rem(me_q + d, nq)).start())

    arrived(recv1.at[pl.ds(0, np_ - 1)], 1)
    mine = pl.multiple_of(me_p * deep, deep)
    for step in range(2):
        for s in range(per):
            slot = lax.rem(me_p - holder(step, me_p + s * np_) - 1 + 2 * np_, np_)
            pivot_row = recv1[slot, pl.ds(step * per + s, 1), :]
            for w in range(wide):
                lanes = slice(w * LANES, (w + 1) * LANES)
                special[pl.ds(mine + (step * per + s) * wide + w, 1), :] = pivot_row[:, lanes]

    own = special.at[pl.ds(mine, deep)]
    each(1, np_, lambda d: remote(own, own, 3, 3, lax.rem(me_p + d, np_), me_q).start())

    @pl.when(me_y > 0)
    def _():
        arrived(panel(me_c, lax.rem(me_y, 4)), 4)
        pass_on_all()
        to_sibling(panel(me_c, lax.rem(me_y, 4)))

    def along_z(ref, send, recv):
        def start(d):
            to = lax.rem(me_z + d, nz) * nx + me_x
            remote(ref.at[me_z], ref.at[me_z], send, recv, to, me_q).start()

        each(1, nz, start)

    for step in range(2):
        @pl.when(me_p != step)
        def _():
            arrived(tops_all.at[0, step], 9 + step)

    along_z(tops_all, 9, 11)

    for c in range(2):
        @pl.when(me_q != c)
        def _():
            arrived(recv_y.at[c], 7 + c)

    pieces[me_z] = recv_y[...]
    along_z(pieces, 8, 2)

    @pl.when(me_y > 0)
    def _():
        arrived(panels.at[me_c, pl.ds(0, 3 * quarter)], 5)
        for k in range(1, 4):
            to_sibling(panel(me_c, lax.rem(me_y + k, 4)))

    arrived(tops_all.at[pl.ds(0, nz - 1)], 11)
    arrived(special.at[pl.ds(0, deep * (np_ - 1))], 3)

    def rows_of(step):
        def part(s, w):
            return special[pl.ds((step * per + s) * wide + w, np_, stride=deep), :]

        return jnp.concatenate(
            [jnp.concatenate([part(s, w) for s in range(per)], 0) for w in range(wide)], 1
        )

    def tops_of(step):
        whole = tops_all[:, step].astype(jnp.float32)
        return jnp.concatenate(
            [whole[:, w * group:(w + 1) * group].reshape(NB, LANES) for w in range(wide)], 1
        )

    pivot0, pivot1, top0, top1 = rows_of(0), rows_of(1), tops_of(0), tops_of(1)
    heads[:NB, :] = pivot0
    heads[NB:2 * NB, :] = dot(lower[0], pivot0, HIGHEST)
    stays = 1.0 - jnp.sum(same, axis=1, keepdims=True)
    heads[2 * NB:, :] = pivot1 * stays + dot(same, top0)
    stays = 1.0 - jnp.sum(low, axis=1, keepdims=True)
    top1 = top1 * stays + dot(low, top0)
    change = jnp.concatenate([top0 - pivot0, top1 - pivot1], 0)
    change = jnp.concatenate(spread(change), 0)
    for begin in range(0, rows, LANES):
        take = put[pl.ds(begin, LANES), :]
        base[pl.ds(begin, LANES), :] += dot(jnp.concatenate([take, take], 1), change)

    arrived(pieces.at[pl.ds(0, nz - 1)], 2)
    arrived(panels.at[1 - me_c], 6)

    sent(send1.at[pl.ds(0, np_ - 1)], 1)
    sent(special.at[pl.ds(0, deep * (np_ - 1))], 3)
    sent(pieces.at[pl.ds(0, nz - 1)], 8)
    sent(tops_all.at[pl.ds(0, nz - 1)], 9)
    sent(panels.at[me_c], 6)

    @pl.when(me_p < 2)
    def _():
        each(1, np_, lambda d: sent(tops.at[0], 2))

    @pl.when(me_y == 0)
    def _():
        sent(recv_z.at[pl.ds(0, np_ - 1)], 0)
        each(1, ny, lambda d: sent(panel(0, 0), 4))
        each(1, nq, lambda d: sent(recv_y.at[0], 7))

    near = (me_y == 1) | (me_y == ny - 1)
    far = (me_y == 2) | (me_y == ny - 2)
    sent(panels.at[0, pl.ds(0, 2 * quarter)], 5)

    @pl.when(~near)
    def _():
        sent(panels.at[0, pl.ds(0, quarter // 2)], 5)

    @pl.when(~(near | far))
    def _():
        sent(panels.at[0, pl.ds(0, quarter // 2)], 5)


def update(np_, nx, base, put, heads, panels, pieces, pivots, lower, upper, out, held, out_sem):
    me_p, me_q = lax.axis_index("prow"), lax.axis_index("pcol")
    rows, cols = base.shape
    height = panels.shape[1]
    group = NB // (np_ // nx)
    pivot0, upper0, head1 = (heads[pl.ds(k * NB, NB), :] for k in range(3))
    lane, row = iota((NB, cols), 1), iota((NB, cols), 0)
    in_panel = lane < NB
    here0, here1 = in_panel & (me_q == 0), in_panel & (me_q == 1)

    _, _, same, low = pivot_maps(pivots)
    stays = 1.0 - jnp.sum(same, axis=1, keepdims=True)
    stays_low = 1.0 - jnp.sum(low, axis=1, keepdims=True)
    same, low = same.astype(BF16), low.astype(BF16)

    def held_of(c):
        both = pieces[:, c].astype(jnp.float32)
        above, below = (both[:, k * group:(k + 1) * group].reshape(NB, LANES) for k in range(2))
        top0, top1 = above[:, NB:], below[:, :NB]
        return above[:, :NB] + below[:, NB:], (top0, top1 * stays_low + dot(low, top0.astype(BF16)))

    (panel_row1, tops0), (panel_row0, tops1) = held_of(0), held_of(1)
    panel_tops = [tops0, tops1]

    left1 = panel_row1 * stays + dot(same, panel_tops[0][0].astype(BF16))
    half0 = upper0.astype(BF16)
    rest1 = head1 - dot(left1.astype(BF16), half0)
    upper1 = dot(lower[1], rest1, HIGHEST)
    half1 = upper1.astype(BF16)

    cross = dot(lower[0], panel_row0, HIGHEST).astype(BF16).astype(jnp.float32)
    cross = dot(cross, upper[1], HIGHEST)
    cross = jnp.concatenate([beside(cross, 0), beside(cross, 1)], 0)
    cross = jnp.concatenate(spread(cross), 0)

    unit = jnp.where(lane == row, -1.0, 0.0).astype(BF16)
    none = jnp.zeros_like(unit)
    right0 = jnp.where(here0, unit, jnp.where(here1, none, half0))
    right1 = jnp.where(here1, unit, jnp.where(here0, none, half1))
    keep = jnp.where((here0 | here1)[:1], 0.0, 1.0)
    rights = (
        jnp.concatenate([right0, none, right1, none], 0),
        jnp.concatenate([none, right0, none, right1], 0),
    )
    ones = jnp.ones((2 * NB, NB), jnp.float32)

    def moved(side):
        parts = [jnp.concatenate(panel_tops[c], 0) for c in range(2)] + [ones]
        return jnp.concatenate([beside(x, side) for x in parts], 1).astype(BF16)

    moved0, moved1 = moved(0), moved(1)
    copies = []
    step = 4 * LANES
    for begin in range(0, height, step):
        size = min(step, height - begin)
        over = max(0, min(size, rows - height - begin))
        both = dot(put[pl.ds(begin, size), :], moved0)
        if over:
            side1 = dot(put[pl.ds(height + begin, over), :], moved1)
            if over < size:
                side1 = jnp.concatenate([side1, jnp.zeros((size - over, 3 * LANES), jnp.float32)], 0)
            both += side1
        stay = 1.0 - both[:, 2 * LANES:]
        panel0 = panels[0, pl.ds(begin, size), :].astype(jnp.float32) * stay + both[:, :LANES]
        panel1 = panels[1, pl.ds(begin, size), :].astype(jnp.float32) * stay + both[:, LANES:2 * LANES]
        panel0 = panel0.astype(BF16)
        panel1 = (panel1 - dot(jnp.concatenate([panel0, panel0], 1), cross)).astype(BF16)
        two = jnp.concatenate([panel0, panel1], 1)
        for side, count in ((0, size), (1, over)):
            if count:
                where = pl.ds(side * height + begin, count)
                value = base[where, :] * keep - dot(two[:count], rights[side])
                if side == 0 and begin == 0:
                    heads0 = jnp.where(here0, pivot0, upper0)
                    wide = jnp.concatenate([left1] * (cols // NB), 1)
                    heads1 = jnp.where(here0, wide, jnp.where(here1, rest1, upper1))
                    head = jnp.where(me_p == 0, heads0, jnp.where(me_p == 1, heads1, value[:NB]))
                    value = jnp.concatenate([head, value[NB:]], 0)
                held[where, :] = value
                copies.append(pltpu.make_async_copy(held.at[where], out.at[where], out_sem.at[len(copies)]))
                copies[-1].start()
    for copy in copies:
        copy.wait()


def local(np_, nx, nq, matrix, pivots, lower_inv, upper_inv):
    rows, cols = matrix.shape
    nz = np_ // nx
    per, group = NB // np_, NB // nz
    height = -(-rows // (2 * LANES)) * LANES
    vmem = pl.BlockSpec(memory_space=pltpu.VMEM)
    smem = pl.BlockSpec(memory_space=pltpu.SMEM)
    anywhere = pl.BlockSpec(memory_space=pl.ANY)
    f32 = jnp.float32
    kept = pl.pallas_call(
        functools.partial(exchange, np_, nx, nq),
        out_shape=(
            jax.ShapeDtypeStruct((rows, cols), f32),
            jax.ShapeDtypeStruct((rows, 2 * NB), BF16),
            jax.ShapeDtypeStruct((3 * NB, cols), f32),
            jax.ShapeDtypeStruct((2, height, LANES), BF16),
            jax.ShapeDtypeStruct((nz, 2, 2 * group, LANES), BF16),
            jax.ShapeDtypeStruct(pivots.shape, jnp.int32),
            jax.ShapeDtypeStruct(lower_inv.shape, f32),
            jax.ShapeDtypeStruct(upper_inv.shape, f32),
        ),
        in_specs=[smem] + [anywhere] * 4,
        out_specs=(vmem,) * 8,
        scratch_shapes=[
            pltpu.VMEM((2 * NB * (cols // LANES), LANES), f32),
            pltpu.VMEM((np_, 2 * per, cols), f32),
            pltpu.VMEM((np_, 2 * per, cols), f32),
            pltpu.VMEM((nz, group * cols // LANES, LANES), BF16),
            pltpu.VMEM((nz, 2, group * cols // LANES, LANES), BF16),
            pltpu.VMEM((nz, group, LANES), f32),
            pltpu.VMEM((np_, group, LANES), f32),
            pltpu.VMEM((group, LANES), f32),
            pltpu.VMEM((2, 2 * group, LANES), BF16),
            pltpu.SemaphoreType.DMA((4,)),
            pltpu.SemaphoreType.DMA((10,)),
            pltpu.SemaphoreType.DMA((12,)),
        ],
        compiler_params=pltpu.CompilerParams(
            collective_id=0, has_side_effects=True, vmem_limit_bytes=VMEM_LIMIT
        ),
    )(pivots, *(pltpu.with_memory_space_constraint(x, pltpu.HBM) for x in (pivots, matrix, lower_inv, upper_inv)))
    return pl.pallas_call(
        functools.partial(update, np_, nx),
        out_shape=jax.ShapeDtypeStruct((rows, cols), f32),
        in_specs=[vmem] * 8,
        out_specs=anywhere,
        scratch_shapes=[pltpu.VMEM((rows, cols), f32), pltpu.SemaphoreType.DMA((2 * height // LANES,))],
        compiler_params=pltpu.CompilerParams(vmem_limit_bytes=VMEM_LIMIT),
    )(*kept)


def solution(mesh):
    np_, nq = mesh.shape["prow"], mesh.shape["pcol"]
    nx = 4 if np_ > 4 else 2
    placed = (P("prow", "pcol"), P(), P(), P())
    return jax.shard_map(
        functools.partial(local, np_, nx, nq),
        mesh=mesh, in_specs=placed, out_specs=P("prow", "pcol"), check_vma=False,
    )
```

```python
import functools

import jax
import jax.numpy as jnp
from jax import lax
from jax.experimental import pallas as pl
from jax.experimental.pallas import tpu as pltpu
from jax.sharding import PartitionSpec as P

NB = 64
LANES = 128
HIGHEST = lax.Precision.HIGHEST
MESH = pl.DeviceIdType.MESH
BF16 = jnp.bfloat16
VMEM_LIMIT = 32 * 1024 * 1024


def dot(a, b, precision=None):
    return jnp.dot(a, b, precision=precision, preferred_element_type=jnp.float32)


def iota(shape, axis):
    return lax.broadcasted_iota(jnp.int32, shape, axis)


def beside(x, side):
    parts = [x, jnp.zeros_like(x)]
    return jnp.concatenate(parts[::-1] if side else parts, 1)


def column(row):
    on = iota((NB, NB), 0) == iota((NB, NB), 1)
    return jnp.sum(jnp.where(on, row, jnp.zeros_like(row)), axis=1, keepdims=True)


def pivot_maps(pivots):
    values = pivots[...].astype(jnp.float32)
    first, second = values[0:1], values[1:2]
    same = (column(second) == first).astype(jnp.float32)
    low = ((NB + iota((NB, NB), 0)).astype(jnp.float32) == first).astype(jnp.float32)
    return first, second, same, low


def spread(x):
    high = x.astype(BF16)
    return high, (x - high.astype(jnp.float32)).astype(BF16)


def three(a):
    high, rest = spread(a)
    return jnp.concatenate([high, rest, high], 1)


def dot3(a3, b):
    high, rest = spread(b)
    return dot(a3, jnp.concatenate([high, high, rest], 0))


def own_columns(me_q, cols):
    in_panel = iota((NB, cols), 1) < NB
    here0, here1 = in_panel & (me_q == 0), in_panel & (me_q == 1)
    return here0, here1, jnp.where((here0 | here1)[:1], 0.0, 1.0)


def own_unit(cols):
    return jnp.where(iota((NB, cols), 1) == iota((NB, cols), 0), -1.0, 0.0).astype(BF16)


def exchange(np_, nx, nq, scalars, pivots_at, matrix, lower_at, upper_at, base, put, heads, panels, pieces, moved, lower3, pivots,
             lower, upper, pieces_t, special, send1, recv1, tops, tops_all, send_z, recv_z, cand, recv_y, send_t, recv_t, recv_ty,
             load_sem, sends, recvs):
    me_p, me_q = lax.axis_index("prow"), lax.axis_index("pcol")
    ny, nz = nq // 2, np_ // nx
    me_y, me_c = lax.div(me_q, 2), lax.rem(me_q, 2)
    me_z, me_x = lax.div(me_p, nx), lax.rem(me_p, nx)
    rows, cols = base.shape
    per, group = NB // np_, NB // nz
    height = panels.shape[1]
    quarter = height // 4
    half, hg = NB // 2, NB // 2 // nz
    wide = cols // LANES
    deep = 2 * per * wide

    def at(p, q):
        return dict(device_id=(p, q), device_id_type=MESH)

    def remote(src, dst, send, recv, p, q):
        return pltpu.make_async_remote_copy(src, dst, sends.at[send], recvs.at[recv], **at(p, q))

    def arrived(ref, recv):
        remote(ref, ref, 0, recv, me_p, me_q).wait_recv()

    def sent(ref, send):
        remote(ref, ref, send, 0, me_p, me_q).wait_send()

    def each(lower_, upper_, do):
        def body(d, _):
            do(d)
            return 0

        lax.fori_loop(lower_, upper_, body, 0)

    def place(step, i):
        value = scalars[step, i]
        block = lax.div(value, NB)
        return lax.div(block, np_) * NB + lax.rem(value, NB)

    def holder(step, i):
        return lax.rem(lax.div(scalars[step, i], NB), np_)

    loads = [
        pltpu.make_async_copy(src, dst, load_sem.at[k])
        for k, (src, dst) in enumerate(((pivots_at, pivots), (matrix, base), (upper_at, upper), (lower_at, lower)))
    ]
    for load in loads:
        load.start()
    barrier = pltpu.get_barrier_semaphore()
    each(1, np_, lambda d: pl.semaphore_signal(barrier, inc=1, **at(lax.rem(me_p + d, np_), me_q)))
    each(1, nq, lambda d: pl.semaphore_signal(barrier, inc=1, **at(me_p, lax.rem(me_q + d, nq))))

    loads[0].wait()
    first, second, same, low = pivot_maps(pivots)
    gone = (first < 2 * NB) | (jnp.sum(same, axis=0, keepdims=True) > 0)
    goal = jnp.concatenate([jnp.where(gone, -1.0, first), second], 1).astype(jnp.int32)
    for begin in range(0, rows, LANES):
        mine_rows = begin + iota((LANES, 2 * NB), 0)
        whole = (lax.div(mine_rows, NB) * np_ + me_p) * NB + lax.rem(mine_rows, NB)
        put[pl.ds(begin, LANES), :] = jnp.where(whole == goal, 1.0, 0.0).astype(BF16)
    for load in loads[1:]:
        load.wait()
    for step in range(2):
        lower3[step] = three(lower[step])

    def fill(r):
        for step in range(2):
            for s in range(per):
                send1[r, pl.ds(step * per + s, 1), :] = base[pl.ds(place(step, r + s * np_), 1), :]

    each(0, np_, fill)
    recv1[np_ - 1] = send1[me_p]

    @pl.when(me_p < 2)
    def _():
        parts = [base[:NB, w * LANES:(w + 1) * LANES].reshape(nz, group, LANES) for w in range(wide)]
        tops[...] = jnp.concatenate(parts, 1).astype(BF16)
        tops_all[me_z, me_p] = tops[me_z]

    @pl.when(me_y == 0)
    def _():
        mine = upper[me_c]
        left, right = beside(mine, 0), beside(mine, 1)

        def fill_z(i):
            cand[pl.ds(i, 1), :] = base[pl.ds(place(1 - me_c, i), 1), :][:, :LANES]

        each(0, NB, fill_z)
        value = dot(cand[:half, :NB], left, HIGHEST) + dot(cand[half:, :NB], right, HIGHEST)
        for z in range(nz):
            send_z[z] = value[z * hg:(z + 1) * hg]
        recv_z[me_p] = send_z[me_z]

        @pl.when(me_p < 2)
        def _():
            value = dot(base[:half, :NB], left, HIGHEST) + dot(base[half:NB, :NB], right, HIGHEST)
            for z in range(nz):
                send_t[z] = value[z * hg:(z + 1) * hg]
            recv_t[me_p] = send_t[me_z]

        for begin in range(0, height, LANES):
            part = dot(base[pl.ds(begin, LANES), :NB], left, HIGHEST)
            if begin + height < rows:
                part += dot(base[pl.ds(height + begin, LANES), :NB], right, HIGHEST)
            panels[me_c, pl.ds(begin, LANES), :] = part.astype(BF16)

    pl.semaphore_wait(barrier, np_ + nq - 2)

    def panel(c, k, begin=0, size=quarter):
        return panels.at[c, pl.ds(pl.multiple_of(k * quarter + begin, 16), size)]

    def pass_on(y, begin, size):
        to = lax.rem(me_y + y + ny, ny)

        @pl.when(to > 0)
        def _():
            part = panel(me_c, lax.rem(me_y, 4), begin, size)
            remote(part, part, 5, 5, me_p, 2 * to + me_c).start()

    def pass_on_all():
        pass_on(2, 0, quarter // 2)
        pass_on(-2, quarter // 2, quarter // 2)
        pass_on(1, 0, quarter)
        pass_on(-1, 0, quarter)

    def to_sibling(part):
        remote(part, part, 6, 6, me_p, 2 * me_y + 1 - me_c).start()

    @pl.when(me_y == 0)
    def _():
        def start_z(d):
            to = lax.rem(me_p + d, np_)
            remote(send_z.at[lax.div(to, nx)], recv_z.at[me_p], 0, 0, to, me_q).start()

        each(1, np_, start_z)

        @pl.when(me_p < 2)
        def _():
            def start_t(d):
                to = lax.rem(me_p + d, np_)
                remote(send_t.at[lax.div(to, nx)], recv_t.at[me_p], 10, 12 + me_p, to, me_q).start()

            each(1, np_, start_t)

        for d in range(ny // 2, 0, -1):
            for y in sorted({d, ny - d}):
                part = panel(me_c, y % 4)
                remote(part, part, 4, 4, me_p, 2 * y + me_c).start()

    def start1(d):
        to = lax.rem(me_p + d, np_)
        remote(send1.at[to], recv1.at[d - 1], 1, 1, to, me_q).start()

    each(1, np_, start1)

    @pl.when(me_p < 2)
    def _():
        def start_top(d):
            to = lax.rem(me_p + d, np_)
            to_z = lax.div(to, nx)
            remote(tops.at[to_z], tops_all.at[to_z, me_p], 2, 9 + me_p, to, me_q).start()

        each(1, np_, start_top)

    @pl.when(me_y == 0)
    def _():
        for step in range(2):
            @pl.when(me_p != step)
            def _():
                arrived(recv_t.at[step], 12 + step)

        recv_ty[me_c] = recv_t[...]
        each(1, nq, lambda d: remote(recv_ty.at[me_c], recv_ty.at[me_c], 11, 14 + me_c,
                                     me_p, lax.rem(me_q + d, nq)).start())
        arrived(recv_z.at[pl.ds(0, np_ - 1)], 0)
        lane = iota((1, LANES), 1)
        for g in range(hg):
            low_row, high_row = (
                recv_z[holder(1 - me_c, me_z * hg + g + k * half), pl.ds(g, 1), :] for k in range(2)
            )
            recv_y[me_c, pl.ds(g, 1), :] = jnp.where(lane < NB, low_row, high_row)
        each(1, nq, lambda d: remote(recv_y.at[me_c], recv_y.at[me_c], 7, 7 + me_c,
                                     me_p, lax.rem(me_q + d, nq)).start())
        pass_on_all()
        to_sibling(panels.at[me_c])

    arrived(recv1.at[pl.ds(0, np_ - 1)], 1)
    mine = pl.multiple_of(me_p * deep, deep)
    for step in range(2):
        for s in range(per):
            slot = lax.rem(me_p - holder(step, me_p + s * np_) - 1 + 2 * np_, np_)
            pivot_row = recv1[slot, pl.ds(step * per + s, 1), :]
            for w in range(wide):
                lanes = slice(w * LANES, (w + 1) * LANES)
                special[pl.ds(mine + (step * per + s) * wide + w, 1), :] = pivot_row[:, lanes]

    own = special.at[pl.ds(mine, deep)]
    each(1, np_, lambda d: remote(own, own, 3, 3, lax.rem(me_p + d, np_), me_q).start())

    @pl.when(me_y > 0)
    def _():
        arrived(panel(me_c, lax.rem(me_y, 4)), 4)
        pass_on_all()
        to_sibling(panel(me_c, lax.rem(me_y, 4)))

    def along_z(ref, send, recv):
        def start(d):
            to = lax.rem(me_z + d, nz) * nx + me_x
            remote(ref.at[me_z], ref.at[me_z], send, recv, to, me_q).start()

        each(1, nz, start)

    for step in range(2):
        @pl.when(me_p != step)
        def _():
            arrived(tops_all.at[0, step], 9 + step)

    along_z(tops_all, 9, 11)

    for c in range(2):
        @pl.when(me_q != c)
        def _():
            arrived(recv_ty.at[c], 14 + c)

    pieces_t[me_z] = jnp.concatenate([recv_ty[c, k] for c in range(2) for k in range(2)], 0).astype(BF16)
    along_z(pieces_t, 12, 16)

    for c in range(2):
        @pl.when(me_q != c)
        def _():
            arrived(recv_y.at[c], 7 + c)

    pieces[me_z] = recv_y[...]
    along_z(pieces, 8, 2)

    @pl.when(me_y > 0)
    def _():
        arrived(panels.at[me_c, pl.ds(0, 3 * quarter)], 5)
        for k in range(1, 4):
            to_sibling(panel(me_c, lax.rem(me_y + k, 4)))

    arrived(tops_all.at[pl.ds(0, nz - 1)], 11)

    def rows_of(step):
        def part(s, w):
            return special[pl.ds((step * per + s) * wide + w, np_, stride=deep), :]

        return jnp.concatenate(
            [jnp.concatenate([part(s, w) for s in range(per)], 0) for w in range(wide)], 1
        )

    def tops_of(step):
        whole = tops_all[:, step].astype(jnp.float32)
        return jnp.concatenate(
            [whole[:, w * group:(w + 1) * group].reshape(NB, LANES) for w in range(wide)], 1
        )

    top0, top1 = tops_of(0), tops_of(1)
    stays = 1.0 - jnp.sum(same, axis=1, keepdims=True)
    stays_low = 1.0 - jnp.sum(low, axis=1, keepdims=True)
    new_head = dot(same, top0)
    top1 = top1 * stays_low + dot(low, top0)
    def move_tops():
        arrived(pieces_t.at[pl.ds(0, nz - 1)], 16)
        whole = pieces_t[...].astype(jnp.float32)

        def panel_tops(c):
            def top(k):
                begin = (2 * c + k) * hg
                packed = jnp.concatenate([whole[z, begin:begin + hg] for z in range(nz)], 0)
                return jnp.concatenate([packed[:, :NB], packed[:, NB:]], 0)

            return top(0), top(1) * stays_low + dot(low, top(0))

        both_tops = [panel_tops(c) for c in range(2)]
        heads[3 * NB:, :] = jnp.concatenate([dot(same, both_tops[0][0])] * (cols // NB), 1)
        ones = jnp.ones((2 * NB, NB), jnp.float32)
        for side in range(2):
            parts = [jnp.concatenate(tops_c, 0) for tops_c in both_tops] + [ones]
            moved[side] = jnp.concatenate([beside(x, side) for x in parts], 1).astype(BF16)

    pl.when(me_y == 0)(move_tops)
    arrived(special.at[pl.ds(0, deep * (np_ - 1))], 3)
    pivot0, pivot1 = rows_of(0), rows_of(1)
    change = jnp.concatenate([top0 - pivot0, top1 - pivot1], 0)
    change = jnp.concatenate(spread(change), 0)
    heads[:NB, :] = pivot0
    heads[NB:2 * NB, :] = dot3(lower3[0], pivot0)
    heads[2 * NB:3 * NB, :] = pivot1 * stays + new_head
    for begin in range(0, rows, LANES):
        take = put[pl.ds(begin, LANES), :]
        base[pl.ds(begin, LANES), :] += dot(jnp.concatenate([take, take], 1), change)

    pl.when(me_y > 0)(move_tops)
    arrived(pieces.at[pl.ds(0, nz - 1)], 2)
    arrived(panels.at[1 - me_c], 6)

    sent(send1.at[pl.ds(0, np_ - 1)], 1)
    sent(special.at[pl.ds(0, deep * (np_ - 1))], 3)
    sent(pieces.at[pl.ds(0, nz - 1)], 8)
    sent(tops_all.at[pl.ds(0, nz - 1)], 9)
    sent(pieces_t.at[pl.ds(0, nz - 1)], 12)
    sent(panels.at[me_c], 6)

    @pl.when(me_p < 2)
    def _():
        each(1, np_, lambda d: sent(tops.at[0], 2))

    @pl.when(me_y == 0)
    def _():
        sent(recv_z.at[pl.ds(0, np_ - 1)], 0)
        each(1, ny, lambda d: sent(panel(0, 0), 4))
        each(1, nq, lambda d: sent(recv_y.at[0], 7))
        each(1, nq, lambda d: sent(recv_ty.at[0], 11))

        @pl.when(me_p < 2)
        def _():
            each(1, np_, lambda d: sent(recv_t.at[0], 10))

    near = (me_y == 1) | (me_y == ny - 1)
    far = (me_y == 2) | (me_y == ny - 2)
    sent(panels.at[0, pl.ds(0, 2 * quarter)], 5)

    @pl.when(~near)
    def _():
        sent(panels.at[0, pl.ds(0, quarter // 2)], 5)

    @pl.when(~(near | far))
    def _():
        sent(panels.at[0, pl.ds(0, quarter // 2)], 5)


def update(base, put, heads, panels, pieces, moved, lower3, pivots, out, held, out_sem):
    me_p, me_q = lax.axis_index("prow"), lax.axis_index("pcol")
    rows, cols = base.shape
    height = panels.shape[1]
    nz = pieces.shape[0]
    pivot0, upper0, head1, left_low = (heads[pl.ds(k * NB, NB), :] for k in range(4))
    here0, here1, keep = own_columns(me_q, cols)
    _, _, same, _ = pivot_maps(pivots)
    stays = 1.0 - jnp.sum(same, axis=1, keepdims=True)

    def unpack(c):
        packed = jnp.concatenate([pieces[z, c] for z in range(nz)], 0)
        return jnp.concatenate([packed[:, :NB], packed[:, NB:]], 0)

    left1 = unpack(0) * stays + left_low[:, :NB]
    rest1 = head1 - dot(left1.astype(BF16), upper0.astype(BF16))
    upper1 = dot3(lower3[1], rest1)

    cross = dot3(lower3[0], unpack(1))
    cross = jnp.concatenate([beside(cross, 0), beside(cross, 1)], 0)
    cross = jnp.concatenate(spread(cross), 0)

    none = jnp.zeros((NB, cols), BF16)
    unit = own_unit(cols)
    right0 = jnp.where(here0, unit, jnp.where(here1, none, upper0.astype(BF16)))
    right1 = jnp.where(here1, unit, jnp.where(here0, none, upper1.astype(BF16)))
    rights = (
        jnp.concatenate([right0, none, right1, none], 0),
        jnp.concatenate([none, right0, none, right1], 0),
    )
    copies = []
    step = 4 * LANES
    for begin in range(0, height, step):
        size = min(step, height - begin)
        over = max(0, min(size, rows - height - begin))
        both = dot(put[pl.ds(begin, size), :], moved[0])
        if over:
            side1 = dot(put[pl.ds(height + begin, over), :], moved[1])
            if over < size:
                side1 = jnp.concatenate([side1, jnp.zeros((size - over, 3 * LANES), jnp.float32)], 0)
            both += side1
        stay = 1.0 - both[:, 2 * LANES:]
        panel0, panel1 = (
            panels[c, pl.ds(begin, size), :].astype(jnp.float32) * stay + both[:, c * LANES:(c + 1) * LANES]
            for c in range(2)
        )
        panel0 = panel0.astype(BF16)
        panel1 = (panel1 - dot(jnp.concatenate([panel0, panel0], 1), cross)).astype(BF16)
        two = jnp.concatenate([panel0, panel1], 1)
        for side, count in ((0, size), (1, over)):
            if count:
                where = pl.ds(side * height + begin, count)
                value = base[where, :] * keep - dot(two[:count], rights[side])
                if side == 0 and begin == 0:
                    heads0 = jnp.where(here0, pivot0, upper0)
                    wide = jnp.concatenate([left1] * (cols // NB), 1)
                    heads1 = jnp.where(here0, wide, jnp.where(here1, rest1, upper1))
                    head = jnp.where(me_p == 0, heads0, jnp.where(me_p == 1, heads1, value[:NB]))
                    value = jnp.concatenate([head, value[NB:]], 0)
                held[where, :] = value
                copies.append(pltpu.make_async_copy(held.at[where], out.at[where], out_sem.at[len(copies)]))
                copies[-1].start()
    for copy in copies:
        copy.wait()


def local(np_, nx, nq, matrix, pivots, lower_inv, upper_inv):
    rows, cols = matrix.shape
    nz = np_ // nx
    per, group = NB // np_, NB // nz
    height = -(-rows // (2 * LANES)) * LANES
    vmem = pl.BlockSpec(memory_space=pltpu.VMEM)
    smem = pl.BlockSpec(memory_space=pltpu.SMEM)
    anywhere = pl.BlockSpec(memory_space=pl.ANY)
    f32 = jnp.float32
    kept = pl.pallas_call(
        functools.partial(exchange, np_, nx, nq),
        out_shape=(
            jax.ShapeDtypeStruct((rows, cols), f32),
            jax.ShapeDtypeStruct((rows, 2 * NB), BF16),
            jax.ShapeDtypeStruct((4 * NB, cols), f32),
            jax.ShapeDtypeStruct((2, height, LANES), BF16),
            jax.ShapeDtypeStruct((nz, 2, group // 2, LANES), f32),
            jax.ShapeDtypeStruct((2, 2 * NB, 3 * LANES), BF16),
            jax.ShapeDtypeStruct((2, NB, 3 * NB), BF16),
            jax.ShapeDtypeStruct(pivots.shape, jnp.int32),
        ),
        in_specs=[smem] + [anywhere] * 4,
        out_specs=(vmem,) * 8,
        scratch_shapes=[
            pltpu.VMEM(lower_inv.shape, f32),
            pltpu.VMEM(upper_inv.shape, f32),
            pltpu.VMEM((nz, 2 * group, LANES), BF16),
            pltpu.VMEM((2 * NB * (cols // LANES), LANES), f32),
            pltpu.VMEM((np_, 2 * per, cols), f32),
            pltpu.VMEM((np_, 2 * per, cols), f32),
            pltpu.VMEM((nz, group * cols // LANES, LANES), BF16),
            pltpu.VMEM((nz, 2, group * cols // LANES, LANES), BF16),
            pltpu.VMEM((nz, group // 2, LANES), f32),
            pltpu.VMEM((np_, group // 2, LANES), f32),
            pltpu.VMEM((NB, LANES), f32),
            pltpu.VMEM((2, group // 2, LANES), f32),
            pltpu.VMEM((nz, group // 2, LANES), f32),
            pltpu.VMEM((2, group // 2, LANES), f32),
            pltpu.VMEM((2, 2, group // 2, LANES), f32),
            pltpu.SemaphoreType.DMA((4,)),
            pltpu.SemaphoreType.DMA((13,)),
            pltpu.SemaphoreType.DMA((17,)),
        ],
        compiler_params=pltpu.CompilerParams(
            collective_id=0, has_side_effects=True, vmem_limit_bytes=VMEM_LIMIT
        ),
    )(pivots, *(pltpu.with_memory_space_constraint(x, pltpu.HBM) for x in (pivots, matrix, lower_inv, upper_inv)))
    return pl.pallas_call(
        update,
        out_shape=jax.ShapeDtypeStruct((rows, cols), f32),
        in_specs=[vmem] * 8,
        out_specs=anywhere,
        scratch_shapes=[pltpu.VMEM((rows, cols), f32), pltpu.SemaphoreType.DMA((2 * height // LANES,))],
        compiler_params=pltpu.CompilerParams(vmem_limit_bytes=VMEM_LIMIT),
    )(*kept)


def solution(mesh):
    np_, nq = mesh.shape["prow"], mesh.shape["pcol"]
    nx = 4 if np_ > 4 else 2
    placed = (P("prow", "pcol"), P(), P(), P())
    return jax.shard_map(
        functools.partial(local, np_, nx, nq),
        mesh=mesh, in_specs=placed, out_specs=P("prow", "pcol"), check_vma=False,
    )
```

```python
import functools

import jax
import jax.numpy as jnp
from jax import lax
from jax.experimental import pallas as pl
from jax.experimental.pallas import tpu as pltpu
from jax.sharding import PartitionSpec as P

NB = 64
LANES = 128
HIGHEST = lax.Precision.HIGHEST
MESH = pl.DeviceIdType.MESH
BF16 = jnp.bfloat16
VMEM_LIMIT = 32 * 1024 * 1024


def dot(a, b, precision=None):
    return jnp.dot(a, b, precision=precision, preferred_element_type=jnp.float32)


def iota(shape, axis):
    return lax.broadcasted_iota(jnp.int32, shape, axis)


def beside(x, side):
    parts = [x, jnp.zeros_like(x)]
    return jnp.concatenate(parts[::-1] if side else parts, 1)


def column(row):
    on = iota((NB, NB), 0) == iota((NB, NB), 1)
    return jnp.sum(jnp.where(on, row, jnp.zeros_like(row)), axis=1, keepdims=True)


def pivot_maps(pivots):
    values = pivots[...].astype(jnp.float32)
    first, second = values[0:1], values[1:2]
    same = (column(second) == first).astype(jnp.float32)
    low = ((NB + iota((NB, NB), 0)).astype(jnp.float32) == first).astype(jnp.float32)
    return first, second, same, low


def spread(x):
    high = x.astype(BF16)
    return high, (x - high.astype(jnp.float32)).astype(BF16)


def three(a):
    high, rest = spread(a)
    return jnp.concatenate([high, rest, high], 1)


def dot3(a3, b):
    high, rest = spread(b)
    return dot(a3, jnp.concatenate([high, high, rest], 0))


def own_columns(me_q, cols):
    in_panel = iota((NB, cols), 1) < NB
    here0, here1 = in_panel & (me_q == 0), in_panel & (me_q == 1)
    return here0, here1, jnp.where((here0 | here1)[:1], 0.0, 1.0)


def own_unit(cols):
    return jnp.where(iota((NB, cols), 1) == iota((NB, cols), 0), -1.0, 0.0).astype(BF16)


def exchange(np_, nx, nq, scalars, pivots_at, matrix, lower_at, upper_at, base, put, heads, panels, pieces, moved, lower3, pivots,
             lower, upper, pieces_t, special, send1, recv1, tops, tops_all, send_z, recv_z, cand, recv_y, send_t, recv_t, recv_ty,
             load_sem, sends, recvs):
    me_p, me_q = lax.axis_index("prow"), lax.axis_index("pcol")
    ny, nz = nq // 2, np_ // nx
    me_y, me_c = lax.div(me_q, 2), lax.rem(me_q, 2)
    me_z, me_x = lax.div(me_p, nx), lax.rem(me_p, nx)
    rows, cols = base.shape
    per, group = NB // np_, NB // nz
    height = panels.shape[1]
    quarter = height // 4
    half, hg = NB // 2, NB // 2 // nz
    wide = cols // LANES
    deep = 2 * per * wide

    def at(p, q):
        return dict(device_id=(p, q), device_id_type=MESH)

    def remote(src, dst, send, recv, p, q):
        return pltpu.make_async_remote_copy(src, dst, sends.at[send], recvs.at[recv], **at(p, q))

    def arrived(ref, recv):
        remote(ref, ref, 0, recv, me_p, me_q).wait_recv()

    def sent(ref, send):
        remote(ref, ref, send, 0, me_p, me_q).wait_send()

    def each(lower_, upper_, do):
        def body(d, _):
            do(d)
            return 0

        lax.fori_loop(lower_, upper_, body, 0)

    def place(step, i):
        value = scalars[step, i]
        block = lax.div(value, NB)
        return lax.div(block, np_) * NB + lax.rem(value, NB)

    def holder(step, i):
        return lax.rem(lax.div(scalars[step, i], NB), np_)

    loads = [
        pltpu.make_async_copy(src, dst, load_sem.at[k])
        for k, (src, dst) in enumerate(((pivots_at, pivots), (matrix, base), (upper_at, upper), (lower_at, lower)))
    ]
    for load in loads:
        load.start()
    barrier = pltpu.get_barrier_semaphore()
    each(1, np_, lambda d: pl.semaphore_signal(barrier, inc=1, **at(lax.rem(me_p + d, np_), me_q)))
    each(1, nq, lambda d: pl.semaphore_signal(barrier, inc=1, **at(me_p, lax.rem(me_q + d, nq))))

    loads[0].wait()
    first, second, same, low = pivot_maps(pivots)
    gone = (first < 2 * NB) | (jnp.sum(same, axis=0, keepdims=True) > 0)
    goal = jnp.concatenate([jnp.where(gone, -1.0, first), second], 1).astype(jnp.int32)
    for begin in range(0, rows, LANES):
        mine_rows = begin + iota((LANES, 2 * NB), 0)
        whole = (lax.div(mine_rows, NB) * np_ + me_p) * NB + lax.rem(mine_rows, NB)
        put[pl.ds(begin, LANES), :] = jnp.where(whole == goal, 1.0, 0.0).astype(BF16)
    for load in loads[1:]:
        load.wait()
    for step in range(2):
        lower3[step] = three(lower[step])

    def fill(r):
        for step in range(2):
            for s in range(per):
                send1[r, pl.ds(step * per + s, 1), :] = base[pl.ds(place(step, r + s * np_), 1), :]

    each(0, np_, fill)
    recv1[np_ - 1] = send1[me_p]

    @pl.when(me_p < 2)
    def _():
        parts = [base[:NB, w * LANES:(w + 1) * LANES].reshape(nz, group, LANES) for w in range(wide)]
        tops[...] = jnp.concatenate(parts, 1).astype(BF16)
        tops_all[me_z, me_p] = tops[me_z]

    @pl.when(me_y == 0)
    def _():
        mine = upper[me_c]
        left, right = beside(mine, 0), beside(mine, 1)

        def fill_z(i):
            cand[pl.ds(i, 1), :] = base[pl.ds(place(1 - me_c, i), 1), :][:, :LANES]

        each(0, NB, fill_z)
        value = dot(cand[:half, :NB], left, HIGHEST) + dot(cand[half:, :NB], right, HIGHEST)
        for z in range(nz):
            send_z[z] = value[z * hg:(z + 1) * hg]
        recv_z[me_p] = send_z[me_z]

        @pl.when(me_p < 2)
        def _():
            value = dot(base[:half, :NB], left, HIGHEST) + dot(base[half:NB, :NB], right, HIGHEST)
            for z in range(nz):
                send_t[z] = value[z * hg:(z + 1) * hg]
            recv_t[me_p] = send_t[me_z]

        for begin in range(0, height, LANES):
            part = dot(base[pl.ds(begin, LANES), :NB], left, HIGHEST)
            if begin + height < rows:
                part += dot(base[pl.ds(height + begin, LANES), :NB], right, HIGHEST)
            panels[me_c, pl.ds(begin, LANES), :] = part.astype(BF16)

    pl.semaphore_wait(barrier, np_ + nq - 2)

    def panel(c, k, begin=0, size=quarter):
        return panels.at[c, pl.ds(pl.multiple_of(k * quarter + begin, 16), size)]

    def pass_on(y, begin, size):
        to = lax.rem(me_y + y + ny, ny)

        @pl.when(to > 0)
        def _():
            part = panel(me_c, lax.rem(me_y, 4), begin, size)
            remote(part, part, 5, 5, me_p, 2 * to + me_c).start()

    def pass_on_all():
        pass_on(2, 0, quarter // 2)
        pass_on(-2, quarter // 2, quarter // 2)
        pass_on(1, 0, quarter)
        pass_on(-1, 0, quarter)

    def to_sibling(part):
        remote(part, part, 6, 6, me_p, 2 * me_y + 1 - me_c).start()

    @pl.when(me_y == 0)
    def _():
        def start_z(d):
            to = lax.rem(me_p + d, np_)
            remote(send_z.at[lax.div(to, nx)], recv_z.at[me_p], 0, 0, to, me_q).start()

        each(1, np_, start_z)

        @pl.when(me_p < 2)
        def _():
            def start_t(d):
                to = lax.rem(me_p + d, np_)
                remote(send_t.at[lax.div(to, nx)], recv_t.at[me_p], 10, 12 + me_p, to, me_q).start()

            each(1, np_, start_t)

        for d in range(ny // 2, 0, -1):
            for y in sorted({d, ny - d}):
                part = panel(me_c, y % 4)
                remote(part, part, 4, 4, me_p, 2 * y + me_c).start()

    def start1(d):
        to = lax.rem(me_p + d, np_)
        remote(send1.at[to], recv1.at[d - 1], 1, 1, to, me_q).start()

    each(1, np_, start1)

    @pl.when(me_p < 2)
    def _():
        def start_top(d):
            to = lax.rem(me_p + d, np_)
            to_z = lax.div(to, nx)
            remote(tops.at[to_z], tops_all.at[to_z, me_p], 2, 9 + me_p, to, me_q).start()

        each(1, np_, start_top)

    @pl.when(me_y == 0)
    def _():
        for step in range(2):
            @pl.when(me_p != step)
            def _():
                arrived(recv_t.at[step], 12 + step)

        recv_ty[me_c] = recv_t[...]
        each(1, nq, lambda d: remote(recv_ty.at[me_c], recv_ty.at[me_c], 11, 14 + me_c,
                                     me_p, lax.rem(me_q + d, nq)).start())
        arrived(recv_z.at[pl.ds(0, np_ - 1)], 0)
        lane = iota((1, LANES), 1)
        for g in range(hg):
            low_row, high_row = (
                recv_z[holder(1 - me_c, me_z * hg + g + k * half), pl.ds(g, 1), :] for k in range(2)
            )
            recv_y[me_c, pl.ds(g, 1), :] = jnp.where(lane < NB, low_row, high_row)
        each(1, nq, lambda d: remote(recv_y.at[me_c], recv_y.at[me_c], 7, 7 + me_c,
                                     me_p, lax.rem(me_q + d, nq)).start())
        pass_on_all()
        to_sibling(panels.at[me_c])

    arrived(recv1.at[pl.ds(0, np_ - 1)], 1)
    mine = pl.multiple_of(me_p * deep, deep)
    for step in range(2):
        for s in range(per):
            slot = lax.rem(me_p - holder(step, me_p + s * np_) - 1 + 2 * np_, np_)
            pivot_row = recv1[slot, pl.ds(step * per + s, 1), :]
            for w in range(wide):
                lanes = slice(w * LANES, (w + 1) * LANES)
                special[pl.ds(mine + (step * per + s) * wide + w, 1), :] = pivot_row[:, lanes]

    own = special.at[pl.ds(mine, deep)]
    each(1, np_, lambda d: remote(own, own, 3, 3, lax.rem(me_p + d, np_), me_q).start())

    @pl.when(me_y > 0)
    def _():
        arrived(panel(me_c, lax.rem(me_y, 4)), 4)
        pass_on_all()
        to_sibling(panel(me_c, lax.rem(me_y, 4)))

    def along_z(ref, send, recv):
        def start(d):
            to = lax.rem(me_z + d, nz) * nx + me_x
            remote(ref.at[me_z], ref.at[me_z], send, recv, to, me_q).start()

        each(1, nz, start)

    for step in range(2):
        @pl.when(me_p != step)
        def _():
            arrived(tops_all.at[0, step], 9 + step)

    along_z(tops_all, 9, 11)

    for c in range(2):
        @pl.when(me_q != c)
        def _():
            arrived(recv_ty.at[c], 14 + c)

    pieces_t[me_z] = jnp.concatenate([recv_ty[c, k] for c in range(2) for k in range(2)], 0).astype(BF16)
    along_z(pieces_t, 12, 16)

    for c in range(2):
        @pl.when(me_q != c)
        def _():
            arrived(recv_y.at[c], 7 + c)

    pieces[me_z] = recv_y[...]
    along_z(pieces, 8, 2)

    @pl.when(me_y > 0)
    def _():
        arrived(panels.at[me_c, pl.ds(0, 3 * quarter)], 5)
        for k in range(1, 4):
            to_sibling(panel(me_c, lax.rem(me_y + k, 4)))

    arrived(tops_all.at[pl.ds(0, nz - 1)], 11)

    def rows_of(step):
        def part(s, w):
            return special[pl.ds((step * per + s) * wide + w, np_, stride=deep), :]

        return jnp.concatenate(
            [jnp.concatenate([part(s, w) for s in range(per)], 0) for w in range(wide)], 1
        )

    def tops_of(step):
        whole = tops_all[:, step].astype(jnp.float32)
        return jnp.concatenate(
            [whole[:, w * group:(w + 1) * group].reshape(NB, LANES) for w in range(wide)], 1
        )

    top0, top1 = tops_of(0), tops_of(1)
    stays = 1.0 - jnp.sum(same, axis=1, keepdims=True)
    stays_low = 1.0 - jnp.sum(low, axis=1, keepdims=True)
    new_head = dot(same, top0)
    top1 = top1 * stays_low + dot(low, top0)
    def move_tops():
        arrived(pieces_t.at[pl.ds(0, nz - 1)], 16)
        whole = pieces_t[...].astype(jnp.float32)

        def panel_tops(c):
            def top(k):
                begin = (2 * c + k) * hg
                packed = jnp.concatenate([whole[z, begin:begin + hg] for z in range(nz)], 0)
                return jnp.concatenate([packed[:, :NB], packed[:, NB:]], 0)

            return top(0), top(1) * stays_low + dot(low, top(0))

        both_tops = [panel_tops(c) for c in range(2)]
        heads[3 * NB:, :] = jnp.concatenate([dot(same, both_tops[0][0])] * (cols // NB), 1)
        ones = jnp.ones((2 * NB, NB), jnp.float32)
        for side in range(2):
            parts = [jnp.concatenate(tops_c, 0) for tops_c in both_tops] + [ones]
            moved[side] = jnp.concatenate([beside(x, side) for x in parts], 1).astype(BF16)

    pl.when(me_y == 0)(move_tops)
    arrived(special.at[pl.ds(0, deep * (np_ - 1))], 3)
    pivot0, pivot1 = rows_of(0), rows_of(1)
    change = jnp.concatenate([top0 - pivot0, top1 - pivot1], 0)
    change = jnp.concatenate(spread(change), 0)
    heads[:NB, :] = pivot0
    heads[NB:2 * NB, :] = dot3(lower3[0], pivot0)
    heads[2 * NB:3 * NB, :] = pivot1 * stays + new_head
    for begin in range(0, rows, LANES):
        take = put[pl.ds(begin, LANES), :]
        base[pl.ds(begin, LANES), :] += dot(jnp.concatenate([take, take], 1), change)

    pl.when(me_y > 0)(move_tops)
    arrived(pieces.at[pl.ds(0, nz - 1)], 2)
    arrived(panels.at[1 - me_c], 6)

    sent(send1.at[pl.ds(0, np_ - 1)], 1)
    sent(special.at[pl.ds(0, deep * (np_ - 1))], 3)
    sent(pieces.at[pl.ds(0, nz - 1)], 8)
    sent(tops_all.at[pl.ds(0, nz - 1)], 9)
    sent(pieces_t.at[pl.ds(0, nz - 1)], 12)
    sent(panels.at[me_c], 6)

    @pl.when(me_p < 2)
    def _():
        each(1, np_, lambda d: sent(tops.at[0], 2))

    @pl.when(me_y == 0)
    def _():
        sent(recv_z.at[pl.ds(0, np_ - 1)], 0)
        each(1, ny, lambda d: sent(panel(0, 0), 4))
        each(1, nq, lambda d: sent(recv_y.at[0], 7))
        each(1, nq, lambda d: sent(recv_ty.at[0], 11))

        @pl.when(me_p < 2)
        def _():
            each(1, np_, lambda d: sent(recv_t.at[0], 10))

    near = (me_y == 1) | (me_y == ny - 1)
    far = (me_y == 2) | (me_y == ny - 2)
    sent(panels.at[0, pl.ds(0, 2 * quarter)], 5)

    @pl.when(~near)
    def _():
        sent(panels.at[0, pl.ds(0, quarter // 2)], 5)

    @pl.when(~(near | far))
    def _():
        sent(panels.at[0, pl.ds(0, quarter // 2)], 5)


def update(base, put, heads, panels, pieces, moved, lower3, pivots, out, held, out_sem):
    me_p, me_q = lax.axis_index("prow"), lax.axis_index("pcol")
    rows, cols = base.shape
    height = panels.shape[1]
    nz = pieces.shape[0]
    pivot0, upper0, head1, left_low = (heads[pl.ds(k * NB, NB), :] for k in range(4))
    here0, here1, keep = own_columns(me_q, cols)
    _, _, same, _ = pivot_maps(pivots)
    stays = 1.0 - jnp.sum(same, axis=1, keepdims=True)

    def unpack(c):
        packed = jnp.concatenate([pieces[z, c] for z in range(nz)], 0)
        return jnp.concatenate([packed[:, :NB], packed[:, NB:]], 0)

    left1 = unpack(0) * stays + left_low[:, :NB]
    rest1 = head1 - dot(left1.astype(BF16), upper0.astype(BF16))
    upper1 = dot3(lower3[1], rest1)

    cross = dot3(lower3[0], unpack(1))
    cross = jnp.concatenate([beside(cross, 0), beside(cross, 1)], 0)
    cross = jnp.concatenate(spread(cross), 0)

    none = jnp.zeros((NB, cols), BF16)
    unit = own_unit(cols)
    right0 = jnp.where(here0, unit, jnp.where(here1, none, upper0.astype(BF16)))
    right1 = jnp.where(here1, unit, jnp.where(here0, none, upper1.astype(BF16)))
    rights = (
        jnp.concatenate([right0, none, right1, none], 0),
        jnp.concatenate([none, right0, none, right1], 0),
    )
    copies = []
    step = 4 * LANES
    for begin in range(0, height, step):
        size = min(step, height - begin)
        over = max(0, min(size, rows - height - begin))
        both = dot(put[pl.ds(begin, size), :], moved[0])
        if over:
            side1 = dot(put[pl.ds(height + begin, over), :], moved[1])
            if over < size:
                side1 = jnp.concatenate([side1, jnp.zeros((size - over, 3 * LANES), jnp.float32)], 0)
            both += side1
        stay = 1.0 - both[:, 2 * LANES:]
        panel0, panel1 = (
            panels[c, pl.ds(begin, size), :].astype(jnp.float32) * stay + both[:, c * LANES:(c + 1) * LANES]
            for c in range(2)
        )
        panel0 = panel0.astype(BF16)
        panel1 = (panel1 - dot(jnp.concatenate([panel0, panel0], 1), cross)).astype(BF16)
        two = jnp.concatenate([panel0, panel1], 1)
        for side, count in ((0, size), (1, over)):
            if count:
                where = pl.ds(side * height + begin, count)
                value = base[where, :] * keep - dot(two[:count], rights[side])
                if side == 0 and begin == 0:
                    heads0 = jnp.where(here0, pivot0, upper0)
                    wide = jnp.concatenate([left1] * (cols // NB), 1)
                    heads1 = jnp.where(here0, wide, jnp.where(here1, rest1, upper1))
                    head = jnp.where(me_p == 0, heads0, jnp.where(me_p == 1, heads1, value[:NB]))
                    value = jnp.concatenate([head, value[NB:]], 0)
                held[where, :] = value
                copies.append(pltpu.make_async_copy(held.at[where], out.at[where], out_sem.at[len(copies)]))
                copies[-1].start()
    for copy in copies:
        copy.wait()


def local(np_, nx, nq, matrix, pivots, lower_inv, upper_inv):
    rows, cols = matrix.shape
    nz = np_ // nx
    per, group = NB // np_, NB // nz
    height = -(-rows // (2 * LANES)) * LANES
    vmem = pl.BlockSpec(memory_space=pltpu.VMEM)
    smem = pl.BlockSpec(memory_space=pltpu.SMEM)
    anywhere = pl.BlockSpec(memory_space=pl.ANY)
    f32 = jnp.float32
    kept = pl.pallas_call(
        functools.partial(exchange, np_, nx, nq),
        out_shape=(
            jax.ShapeDtypeStruct((rows, cols), f32),
            jax.ShapeDtypeStruct((rows, 2 * NB), BF16),
            jax.ShapeDtypeStruct((4 * NB, cols), f32),
            jax.ShapeDtypeStruct((2, height, LANES), BF16),
            jax.ShapeDtypeStruct((nz, 2, group // 2, LANES), f32),
            jax.ShapeDtypeStruct((2, 2 * NB, 3 * LANES), BF16),
            jax.ShapeDtypeStruct((2, NB, 3 * NB), BF16),
            jax.ShapeDtypeStruct(pivots.shape, jnp.int32),
        ),
        in_specs=[smem] + [anywhere] * 4,
        out_specs=(vmem,) * 8,
        scratch_shapes=[
            pltpu.VMEM(lower_inv.shape, f32),
            pltpu.VMEM(upper_inv.shape, f32),
            pltpu.VMEM((nz, 2 * group, LANES), BF16),
            pltpu.VMEM((2 * NB * (cols // LANES) + 8, LANES), f32),
            pltpu.VMEM((np_, 2 * per, cols), f32),
            pltpu.VMEM((np_, 2 * per, cols), f32),
            pltpu.VMEM((nz, group * cols // LANES, LANES), BF16),
            pltpu.VMEM((nz, 2, group * cols // LANES, LANES), BF16),
            pltpu.VMEM((nz, group // 2, LANES), f32),
            pltpu.VMEM((np_, group // 2, LANES), f32),
            pltpu.VMEM((NB, LANES), f32),
            pltpu.VMEM((2, group // 2, LANES), f32),
            pltpu.VMEM((nz, group // 2, LANES), f32),
            pltpu.VMEM((2, group // 2, LANES), f32),
            pltpu.VMEM((2, 2, group // 2, LANES), f32),
            pltpu.SemaphoreType.DMA((4,)),
            pltpu.SemaphoreType.DMA((13,)),
            pltpu.SemaphoreType.DMA((17,)),
        ],
        compiler_params=pltpu.CompilerParams(
            collective_id=0, has_side_effects=True, vmem_limit_bytes=VMEM_LIMIT
        ),
    )(pivots, *(pltpu.with_memory_space_constraint(x, pltpu.HBM) for x in (pivots, matrix, lower_inv, upper_inv)))
    return pl.pallas_call(
        update,
        out_shape=jax.ShapeDtypeStruct((rows, cols), f32),
        in_specs=[vmem] * 8,
        out_specs=anywhere,
        scratch_shapes=[pltpu.VMEM((rows, cols), f32), pltpu.SemaphoreType.DMA((2 * height // LANES,))],
        compiler_params=pltpu.CompilerParams(vmem_limit_bytes=VMEM_LIMIT),
    )(*kept)


def solution(mesh):
    np_, nq = mesh.shape["prow"], mesh.shape["pcol"]
    nx = 4 if np_ > 4 else 2
    placed = (P("prow", "pcol"), P(), P(), P())
    return jax.shard_map(
        functools.partial(local, np_, nx, nq),
        mesh=mesh, in_specs=placed, out_specs=P("prow", "pcol"), check_vma=False,
    )
```

```python
import functools

import jax
import jax.numpy as jnp
from jax import lax
from jax.experimental import pallas as pl
from jax.experimental.pallas import tpu as pltpu
from jax.sharding import PartitionSpec as P

NB = 64
LANES = 128
HIGHEST = lax.Precision.HIGHEST
MESH = pl.DeviceIdType.MESH
BF16 = jnp.bfloat16
VMEM_LIMIT = 32 * 1024 * 1024


def dot(a, b, precision=None):
    return jnp.dot(a, b, precision=precision, preferred_element_type=jnp.float32)


def iota(shape, axis):
    return lax.broadcasted_iota(jnp.int32, shape, axis)


def beside(x, side):
    parts = [x, jnp.zeros_like(x)]
    return jnp.concatenate(parts[::-1] if side else parts, 1)


def column(row):
    on = iota((NB, NB), 0) == iota((NB, NB), 1)
    return jnp.sum(jnp.where(on, row, jnp.zeros_like(row)), axis=1, keepdims=True)


def pivot_maps(pivots):
    values = pivots[...].astype(jnp.float32)
    first, second = values[0:1], values[1:2]
    same = (column(second) == first).astype(jnp.float32)
    low = ((NB + iota((NB, NB), 0)).astype(jnp.float32) == first).astype(jnp.float32)
    return first, second, same, low


def spread(x):
    high = x.astype(BF16)
    return high, (x - high.astype(jnp.float32)).astype(BF16)


def three(a):
    high, rest = spread(a)
    return jnp.concatenate([high, rest, high], 1)


def dot3(a3, b):
    high, rest = spread(b)
    return dot(a3, jnp.concatenate([high, high, rest], 0))


def own_columns(me_q, cols):
    in_panel = iota((NB, cols), 1) < NB
    here0, here1 = in_panel & (me_q == 0), in_panel & (me_q == 1)
    return here0, here1, jnp.where((here0 | here1)[:1], 0.0, 1.0)


def own_unit(cols):
    return jnp.where(iota((NB, cols), 1) == iota((NB, cols), 0), -1.0, 0.0).astype(BF16)


def exchange(np_, nx, nq, scalars, pivots_at, matrix, lower_at, upper_at, base, put, heads, panels, pieces, moved, lower3, pivots,
             lower, upper, pieces_t, special, send1, recv1, tops, tops_all, send_z, recv_z, cand, recv_y, send_t, recv_t, recv_ty,
             load_sem, sends, recvs):
    me_p, me_q = lax.axis_index("prow"), lax.axis_index("pcol")
    ny, nz = nq // 2, np_ // nx
    me_y, me_c = lax.div(me_q, 2), lax.rem(me_q, 2)
    me_z, me_x = lax.div(me_p, nx), lax.rem(me_p, nx)
    rows, cols = base.shape
    per, group = NB // np_, NB // nz
    height = panels.shape[1]
    quarter = height // 4
    half, hg = NB // 2, NB // 2 // nz
    wide = cols // LANES
    deep = 2 * per * wide

    def at(p, q):
        return dict(device_id=(p, q), device_id_type=MESH)

    def remote(src, dst, send, recv, p, q):
        return pltpu.make_async_remote_copy(src, dst, sends.at[send], recvs.at[recv], **at(p, q))

    def arrived(ref, recv):
        remote(ref, ref, 0, recv, me_p, me_q).wait_recv()

    def sent(ref, send):
        remote(ref, ref, send, 0, me_p, me_q).wait_send()

    def each(lower_, upper_, do):
        def body(d, _):
            do(d)
            return 0

        lax.fori_loop(lower_, upper_, body, 0)

    def each_other(count, do):
        def body(d, _):
            away = lax.div(d, 2)
            do(count // 2 + jnp.where(lax.rem(d, 2) == 0, away, -away))
            return 0

        lax.fori_loop(1, count, body, 0)

    def place(step, i):
        value = scalars[step, i]
        block = lax.div(value, NB)
        return lax.div(block, np_) * NB + lax.rem(value, NB)

    def holder(step, i):
        return lax.rem(lax.div(scalars[step, i], NB), np_)

    loads = [
        pltpu.make_async_copy(src, dst, load_sem.at[k])
        for k, (src, dst) in enumerate(((pivots_at, pivots), (matrix, base), (upper_at, upper), (lower_at, lower)))
    ]
    for load in loads:
        load.start()
    barrier = pltpu.get_barrier_semaphore()
    each_other(np_, lambda d: pl.semaphore_signal(barrier, inc=1, **at(lax.rem(me_p + d, np_), me_q)))
    each_other(nq, lambda d: pl.semaphore_signal(barrier, inc=1, **at(me_p, lax.rem(me_q + d, nq))))

    loads[0].wait()
    first, second, same, low = pivot_maps(pivots)
    gone = (first < 2 * NB) | (jnp.sum(same, axis=0, keepdims=True) > 0)
    goal = jnp.concatenate([jnp.where(gone, -1.0, first), second], 1).astype(jnp.int32)
    for begin in range(0, rows, LANES):
        mine_rows = begin + iota((LANES, 2 * NB), 0)
        whole = (lax.div(mine_rows, NB) * np_ + me_p) * NB + lax.rem(mine_rows, NB)
        put[pl.ds(begin, LANES), :] = jnp.where(whole == goal, 1.0, 0.0).astype(BF16)
    for load in loads[1:]:
        load.wait()
    for step in range(2):
        lower3[step] = three(lower[step])

    def fill(r):
        for step in range(2):
            for s in range(per):
                send1[r, pl.ds(step * per + s, 1), :] = base[pl.ds(place(step, r + s * np_), 1), :]

    each(0, np_, fill)
    recv1[np_ - 1] = send1[me_p]

    @pl.when(me_p < 2)
    def _():
        parts = [base[:NB, w * LANES:(w + 1) * LANES].reshape(nz, group, LANES) for w in range(wide)]
        tops[...] = jnp.concatenate(parts, 1).astype(BF16)
        tops_all[me_z, me_p] = tops[me_z]

    @pl.when(me_y == 0)
    def _():
        mine = upper[me_c]
        left, right = beside(mine, 0), beside(mine, 1)

        def fill_z(i):
            cand[pl.ds(i, 1), :] = base[pl.ds(place(1 - me_c, i), 1), :][:, :LANES]

        each(0, NB, fill_z)
        value = dot(cand[:half, :NB], left, HIGHEST) + dot(cand[half:, :NB], right, HIGHEST)
        for z in range(nz):
            send_z[z] = value[z * hg:(z + 1) * hg]
        recv_z[me_p] = send_z[me_z]

        @pl.when(me_p < 2)
        def _():
            value = dot(base[:half, :NB], left, HIGHEST) + dot(base[half:NB, :NB], right, HIGHEST)
            for z in range(nz):
                send_t[z] = value[z * hg:(z + 1) * hg]
            recv_t[me_p] = send_t[me_z]

        for begin in range(0, height, LANES):
            part = dot(base[pl.ds(begin, LANES), :NB], left, HIGHEST)
            if begin + height < rows:
                part += dot(base[pl.ds(height + begin, LANES), :NB], right, HIGHEST)
            panels[me_c, pl.ds(begin, LANES), :] = part.astype(BF16)

    pl.semaphore_wait(barrier, np_ + nq - 2)

    def panel(c, k, begin=0, size=quarter):
        return panels.at[c, pl.ds(pl.multiple_of(k * quarter + begin, 16), size)]

    def pass_on(y, begin, size):
        to = lax.rem(me_y + y + ny, ny)

        @pl.when(to > 0)
        def _():
            part = panel(me_c, lax.rem(me_y, 4), begin, size)
            remote(part, part, 5, 5, me_p, 2 * to + me_c).start()

    def pass_on_all():
        pass_on(2, 0, quarter // 2)
        pass_on(-2, quarter // 2, quarter // 2)
        pass_on(1, 0, quarter)
        pass_on(-1, 0, quarter)

    def to_sibling(part):
        remote(part, part, 6, 6, me_p, 2 * me_y + 1 - me_c).start()

    @pl.when(me_y == 0)
    def _():
        def start_z(d):
            to = lax.rem(me_p + d, np_)
            remote(send_z.at[lax.div(to, nx)], recv_z.at[me_p], 0, 0, to, me_q).start()

        each(1, np_, start_z)

        @pl.when(me_p < 2)
        def _():
            def start_t(d):
                to = lax.rem(me_p + d, np_)
                remote(send_t.at[lax.div(to, nx)], recv_t.at[me_p], 10, 12 + me_p, to, me_q).start()

            each(1, np_, start_t)

        for d in range(ny // 2, 0, -1):
            for y in sorted({d, ny - d}):
                part = panel(me_c, y % 4)
                remote(part, part, 4, 4, me_p, 2 * y + me_c).start()

    def start1(d):
        to = lax.rem(me_p + d, np_)
        remote(send1.at[to], recv1.at[d - 1], 1, 1, to, me_q).start()

    each(1, np_, start1)

    @pl.when(me_p < 2)
    def _():
        def start_top(d):
            to = lax.rem(me_p + d, np_)
            to_z = lax.div(to, nx)
            remote(tops.at[to_z], tops_all.at[to_z, me_p], 2, 9 + me_p, to, me_q).start()

        each(1, np_, start_top)

    @pl.when(me_y == 0)
    def _():
        for step in range(2):
            @pl.when(me_p != step)
            def _():
                arrived(recv_t.at[step], 12 + step)

        recv_ty[me_c] = recv_t[...]
        each_other(nq, lambda d: remote(recv_ty.at[me_c], recv_ty.at[me_c], 11, 14 + me_c,
                                     me_p, lax.rem(me_q + d, nq)).start())
        arrived(recv_z.at[pl.ds(0, np_ - 1)], 0)
        lane = iota((1, LANES), 1)
        for g in range(hg):
            low_row, high_row = (
                recv_z[holder(1 - me_c, me_z * hg + g + k * half), pl.ds(g, 1), :] for k in range(2)
            )
            recv_y[me_c, pl.ds(g, 1), :] = jnp.where(lane < NB, low_row, high_row)
        each_other(nq, lambda d: remote(recv_y.at[me_c], recv_y.at[me_c], 7, 7 + me_c,
                                     me_p, lax.rem(me_q + d, nq)).start())
        pass_on_all()
        to_sibling(panels.at[me_c])

    arrived(recv1.at[pl.ds(0, np_ - 1)], 1)
    mine = pl.multiple_of(me_p * deep, deep)
    for step in range(2):
        for s in range(per):
            slot = lax.rem(me_p - holder(step, me_p + s * np_) - 1 + 2 * np_, np_)
            pivot_row = recv1[slot, pl.ds(step * per + s, 1), :]
            for w in range(wide):
                lanes = slice(w * LANES, (w + 1) * LANES)
                special[pl.ds(mine + (step * per + s) * wide + w, 1), :] = pivot_row[:, lanes]

    own = special.at[pl.ds(mine, deep)]
    each(1, np_, lambda d: remote(own, own, 3, 3, lax.rem(me_p + d, np_), me_q).start())

    @pl.when(me_y > 0)
    def _():
        arrived(panel(me_c, lax.rem(me_y, 4)), 4)
        pass_on_all()
        to_sibling(panel(me_c, lax.rem(me_y, 4)))

    def along_z(ref, send, recv):
        def start(d):
            to = lax.rem(me_z + d, nz) * nx + me_x
            remote(ref.at[me_z], ref.at[me_z], send, recv, to, me_q).start()

        each_other(nz, start)

    for step in range(2):
        @pl.when(me_p != step)
        def _():
            arrived(tops_all.at[0, step], 9 + step)

    along_z(tops_all, 9, 11)

    for c in range(2):
        @pl.when(me_q != c)
        def _():
            arrived(recv_ty.at[c], 14 + c)

    pieces_t[me_z] = jnp.concatenate([recv_ty[c, k] for c in range(2) for k in range(2)], 0).astype(BF16)
    along_z(pieces_t, 12, 16)

    for c in range(2):
        @pl.when(me_q != c)
        def _():
            arrived(recv_y.at[c], 7 + c)

    pieces[me_z] = recv_y[...]
    along_z(pieces, 8, 2)

    @pl.when(me_y > 0)
    def _():
        arrived(panels.at[me_c, pl.ds(0, 3 * quarter)], 5)
        for k in range(1, 4):
            to_sibling(panel(me_c, lax.rem(me_y + k, 4)))

    arrived(tops_all.at[pl.ds(0, nz - 1)], 11)

    def rows_of(step):
        def part(s, w):
            return special[pl.ds((step * per + s) * wide + w, np_, stride=deep), :]

        return jnp.concatenate(
            [jnp.concatenate([part(s, w) for s in range(per)], 0) for w in range(wide)], 1
        )

    def tops_of(step):
        whole = tops_all[:, step].astype(jnp.float32)
        return jnp.concatenate(
            [whole[:, w * group:(w + 1) * group].reshape(NB, LANES) for w in range(wide)], 1
        )

    top0, top1 = tops_of(0), tops_of(1)
    stays = 1.0 - jnp.sum(same, axis=1, keepdims=True)
    stays_low = 1.0 - jnp.sum(low, axis=1, keepdims=True)
    new_head = dot(same, top0)
    top1 = top1 * stays_low + dot(low, top0)
    def move_tops():
        arrived(pieces_t.at[pl.ds(0, nz - 1)], 16)
        whole = pieces_t[...].astype(jnp.float32)

        def panel_tops(c):
            def top(k):
                begin = (2 * c + k) * hg
                packed = jnp.concatenate([whole[z, begin:begin + hg] for z in range(nz)], 0)
                return jnp.concatenate([packed[:, :NB], packed[:, NB:]], 0)

            return top(0), top(1) * stays_low + dot(low, top(0))

        both_tops = [panel_tops(c) for c in range(2)]
        heads[3 * NB:, :] = jnp.concatenate([dot(same, both_tops[0][0])] * (cols // NB), 1)
        ones = jnp.ones((2 * NB, NB), jnp.float32)
        for side in range(2):
            parts = [jnp.concatenate(tops_c, 0) for tops_c in both_tops] + [ones]
            moved[side] = jnp.concatenate([beside(x, side) for x in parts], 1).astype(BF16)

    pl.when(me_y == 0)(move_tops)
    arrived(special.at[pl.ds(0, deep * (np_ - 1))], 3)
    pivot0, pivot1 = rows_of(0), rows_of(1)
    change = jnp.concatenate([top0 - pivot0, top1 - pivot1], 0)
    change = jnp.concatenate(spread(change), 0)
    heads[:NB, :] = pivot0
    heads[NB:2 * NB, :] = dot3(lower3[0], pivot0)
    heads[2 * NB:3 * NB, :] = pivot1 * stays + new_head
    for begin in range(0, rows, LANES):
        take = put[pl.ds(begin, LANES), :]
        base[pl.ds(begin, LANES), :] += dot(jnp.concatenate([take, take], 1), change)

    pl.when(me_y > 0)(move_tops)
    arrived(pieces.at[pl.ds(0, nz - 1)], 2)
    arrived(panels.at[1 - me_c], 6)

    sent(send1.at[pl.ds(0, np_ - 1)], 1)
    sent(special.at[pl.ds(0, deep * (np_ - 1))], 3)
    sent(pieces.at[pl.ds(0, nz - 1)], 8)
    sent(tops_all.at[pl.ds(0, nz - 1)], 9)
    sent(pieces_t.at[pl.ds(0, nz - 1)], 12)
    sent(panels.at[me_c], 6)

    @pl.when(me_p < 2)
    def _():
        each(1, np_, lambda d: sent(tops.at[0], 2))

    @pl.when(me_y == 0)
    def _():
        sent(recv_z.at[pl.ds(0, np_ - 1)], 0)
        each(1, ny, lambda d: sent(panel(0, 0), 4))
        each(1, nq, lambda d: sent(recv_y.at[0], 7))
        each(1, nq, lambda d: sent(recv_ty.at[0], 11))

        @pl.when(me_p < 2)
        def _():
            each(1, np_, lambda d: sent(recv_t.at[0], 10))

    near = (me_y == 1) | (me_y == ny - 1)
    far = (me_y == 2) | (me_y == ny - 2)
    sent(panels.at[0, pl.ds(0, 2 * quarter)], 5)

    @pl.when(~near)
    def _():
        sent(panels.at[0, pl.ds(0, quarter // 2)], 5)

    @pl.when(~(near | far))
    def _():
        sent(panels.at[0, pl.ds(0, quarter // 2)], 5)


def update(base, put, heads, panels, pieces, moved, lower3, pivots, out, held, out_sem):
    me_p, me_q = lax.axis_index("prow"), lax.axis_index("pcol")
    rows, cols = base.shape
    height = panels.shape[1]
    nz = pieces.shape[0]
    pivot0, upper0, head1, left_low = (heads[pl.ds(k * NB, NB), :] for k in range(4))
    here0, here1, keep = own_columns(me_q, cols)
    _, _, same, _ = pivot_maps(pivots)
    stays = 1.0 - jnp.sum(same, axis=1, keepdims=True)

    def unpack(c):
        packed = jnp.concatenate([pieces[z, c] for z in range(nz)], 0)
        return jnp.concatenate([packed[:, :NB], packed[:, NB:]], 0)

    left1 = unpack(0) * stays + left_low[:, :NB]
    rest1 = head1 - dot(left1.astype(BF16), upper0.astype(BF16))
    upper1 = dot3(lower3[1], rest1)

    cross = dot3(lower3[0], unpack(1))
    cross = jnp.concatenate([beside(cross, 0), beside(cross, 1)], 0)
    cross = jnp.concatenate(spread(cross), 0)

    none = jnp.zeros((NB, cols), BF16)
    unit = own_unit(cols)
    right0 = jnp.where(here0, unit, jnp.where(here1, none, upper0.astype(BF16)))
    right1 = jnp.where(here1, unit, jnp.where(here0, none, upper1.astype(BF16)))
    rights = (
        jnp.concatenate([right0, none, right1, none], 0),
        jnp.concatenate([none, right0, none, right1], 0),
    )
    copies = []
    step = 4 * LANES
    for begin in range(0, height, step):
        size = min(step, height - begin)
        over = max(0, min(size, rows - height - begin))
        both = dot(put[pl.ds(begin, size), :], moved[0])
        if over:
            side1 = dot(put[pl.ds(height + begin, over), :], moved[1])
            if over < size:
                side1 = jnp.concatenate([side1, jnp.zeros((size - over, 3 * LANES), jnp.float32)], 0)
            both += side1
        stay = 1.0 - both[:, 2 * LANES:]
        panel0, panel1 = (
            panels[c, pl.ds(begin, size), :].astype(jnp.float32) * stay + both[:, c * LANES:(c + 1) * LANES]
            for c in range(2)
        )
        panel0 = panel0.astype(BF16)
        panel1 = (panel1 - dot(jnp.concatenate([panel0, panel0], 1), cross)).astype(BF16)
        two = jnp.concatenate([panel0, panel1], 1)
        for side, count in ((0, size), (1, over)):
            if count:
                where = pl.ds(side * height + begin, count)
                value = base[where, :] * keep - dot(two[:count], rights[side])
                if side == 0 and begin == 0:
                    heads0 = jnp.where(here0, pivot0, upper0)
                    wide = jnp.concatenate([left1] * (cols // NB), 1)
                    heads1 = jnp.where(here0, wide, jnp.where(here1, rest1, upper1))
                    head = jnp.where(me_p == 0, heads0, jnp.where(me_p == 1, heads1, value[:NB]))
                    value = jnp.concatenate([head, value[NB:]], 0)
                held[where, :] = value
                copies.append(pltpu.make_async_copy(held.at[where], out.at[where], out_sem.at[len(copies)]))
                copies[-1].start()
    for copy in copies:
        copy.wait()


def local(np_, nx, nq, matrix, pivots, lower_inv, upper_inv):
    rows, cols = matrix.shape
    nz = np_ // nx
    per, group = NB // np_, NB // nz
    height = -(-rows // (2 * LANES)) * LANES
    vmem = pl.BlockSpec(memory_space=pltpu.VMEM)
    smem = pl.BlockSpec(memory_space=pltpu.SMEM)
    anywhere = pl.BlockSpec(memory_space=pl.ANY)
    f32 = jnp.float32
    kept = pl.pallas_call(
        functools.partial(exchange, np_, nx, nq),
        out_shape=(
            jax.ShapeDtypeStruct((rows, cols), f32),
            jax.ShapeDtypeStruct((rows, 2 * NB), BF16),
            jax.ShapeDtypeStruct((4 * NB, cols), f32),
            jax.ShapeDtypeStruct((2, height, LANES), BF16),
            jax.ShapeDtypeStruct((nz, 2, group // 2, LANES), f32),
            jax.ShapeDtypeStruct((2, 2 * NB, 3 * LANES), BF16),
            jax.ShapeDtypeStruct((2, NB, 3 * NB), BF16),
            jax.ShapeDtypeStruct(pivots.shape, jnp.int32),
        ),
        in_specs=[smem] + [anywhere] * 4,
        out_specs=(vmem,) * 8,
        scratch_shapes=[
            pltpu.VMEM(lower_inv.shape, f32),
            pltpu.VMEM(upper_inv.shape, f32),
            pltpu.VMEM((nz, 2 * group, LANES), BF16),
            pltpu.VMEM((2 * NB * (cols // LANES) + 8, LANES), f32),
            pltpu.VMEM((np_, 2 * per, cols), f32),
            pltpu.VMEM((np_, 2 * per, cols), f32),
            pltpu.VMEM((nz, group * cols // LANES, LANES), BF16),
            pltpu.VMEM((nz, 2, group * cols // LANES, LANES), BF16),
            pltpu.VMEM((nz, group // 2, LANES), f32),
            pltpu.VMEM((np_, group // 2, LANES), f32),
            pltpu.VMEM((NB, LANES), f32),
            pltpu.VMEM((2, group // 2, LANES), f32),
            pltpu.VMEM((nz, group // 2, LANES), f32),
            pltpu.VMEM((2, group // 2, LANES), f32),
            pltpu.VMEM((2, 2, group // 2, LANES), f32),
            pltpu.SemaphoreType.DMA((4,)),
            pltpu.SemaphoreType.DMA((13,)),
            pltpu.SemaphoreType.DMA((17,)),
        ],
        compiler_params=pltpu.CompilerParams(
            collective_id=0, has_side_effects=True, vmem_limit_bytes=VMEM_LIMIT
        ),
    )(pivots, *(pltpu.with_memory_space_constraint(x, pltpu.HBM) for x in (pivots, matrix, lower_inv, upper_inv)))
    return pl.pallas_call(
        update,
        out_shape=jax.ShapeDtypeStruct((rows, cols), f32),
        in_specs=[vmem] * 8,
        out_specs=anywhere,
        scratch_shapes=[pltpu.VMEM((rows, cols), f32), pltpu.SemaphoreType.DMA((2 * height // LANES,))],
        compiler_params=pltpu.CompilerParams(vmem_limit_bytes=VMEM_LIMIT),
    )(*kept)


def solution(mesh):
    np_, nq = mesh.shape["prow"], mesh.shape["pcol"]
    nx = 4 if np_ > 4 else 2
    placed = (P("prow", "pcol"), P(), P(), P())
    return jax.shard_map(
        functools.partial(local, np_, nx, nq),
        mesh=mesh, in_specs=placed, out_specs=P("prow", "pcol"), check_vma=False,
    )
```
